32 devices in a mesh: rows: 8 (over z, y), heads: 4 (over x, core).
Axes of the slice: x: 2, y: 2, z: 4, core: 2. Of those that a mesh axis runs over, the one named last changes fastest.
Arguments:
- imagery: bfloat16 [5, 512, 1024], P(None, 'rows'), may hold values from -120 to 120
- stem_weight: bfloat16 [11520, 1024], P('rows', 'heads'), may hold values from -0.0546875 to 0.0546875
- token_gain: bfloat16 [1024], replicated, may hold values from 0.099609375 to 1.8984375
- latents: bfloat16 [512, 1024], replicated, may hold values from -6 to 6
- latent_gain: bfloat16 [1024], replicated, may hold values from 0.099609375 to 1.8984375
- query_weight: bfloat16 [1024, 1024], P('rows', 'heads'), may hold values from -1.5 to 1.5
- key_weight: bfloat16 [1024, 1024], P('rows', 'heads'), may hold values from -1.5 to 1.5
- value_weight: bfloat16 [1024, 1024], P('rows', 'heads'), may hold values from -0.1875 to 0.1875
- out_weight: bfloat16 [1024, 1024], P('rows', 'heads'), may hold values from -0.1875 to 0.1875
Outputs:
- latent_out: bfloat16 [512, 1024], P('rows', 'heads')
The draws below stay inside these ranges and needn't reach their ends.
All inputs are finite; a program needn't handle non-finite values.
Results may differ from the reference program's by a relative error of at most 0.035.
The reference program's roundings to bfloat16 on the way (of `patches`, `feature`, `token_norm`, `keys`, `values`, `latent_norm`, `queries` and `mixed`) count: a program that leaves them out, or rounds other values in their place, can miss the bound.
Values may be sent and summed in bfloat16 or wider, within the bound.
A program may use at most 192 MiB of HBM per device.

```python
import math
import jax
import jax.numpy as jnp
from jax import lax

D = 1024
HEADS = 16
LAT = 512
BANDS = 5
KER = 48
STRIDE = 32
KDIM = 11520
TROWS = 2
TCOLS = 32
PIX_ROWS = 512
PIX_COLS = 1024


def projection_base(key):
    return jnp.clip(jax.random.normal(key, (D, D), jnp.float32), -4.0, 4.0) * (1.7 / math.sqrt(D))


def draw_query_weight(key, part):
    key = jax.random.fold_in(key, 11)
    return projection_base(key).astype(jnp.bfloat16)


def draw_key_weight(key, part):
    key = jax.random.fold_in(key, 12)
    return projection_base(key).astype(jnp.bfloat16)


def draw_imagery(key, part):
    key = jax.random.fold_in(key, 13)
    shape = (BANDS, PIX_ROWS, PIX_COLS)
    row_scale = jnp.exp(jax.random.uniform(jax.random.fold_in(key, 1), (BANDS, PIX_ROWS, 1), jnp.float32, 0.0, math.log(10.0)))
    column_scale = jnp.exp(jax.random.uniform(jax.random.fold_in(key, 2), (BANDS, 1, PIX_COLS), jnp.float32, 0.0, math.log(3.0)))
    noise = jnp.clip(jax.random.normal(jax.random.fold_in(key, 3), shape, jnp.float32), -4.0, 4.0)
    return (noise * row_scale * column_scale).astype(jnp.bfloat16)


def shard_levels(rng, extent, cuts, least, largest):
    def one(axis_at, parts):
        draws = jax.random.uniform(jax.random.fold_in(jax.random.fold_in(rng, 6), axis_at), (parts,), jnp.float32, least / len(cuts), largest / len(cuts))
        return jnp.repeat(jnp.exp(draws), extent[axis_at] // parts).reshape((-1,) + (1,) * (len(extent) - axis_at - 1))

    gain = one(*cuts[0])
    for cut in cuts[1:]:
        gain = gain * one(*cut)
    return gain


def normal_values(stream_key, extent, scale, most, split=(), held_as=jnp.bfloat16):
    drawn = jax.random.normal(stream_key, extent, jnp.float32) * scale
    if len(split) > 0:
        drawn = shard_levels(stream_key, extent, split, -0.22, 0.18) * drawn
    return jnp.clip(drawn, min=-most, max=most).astype(held_as)


def setup_inputs(seed: int = 0) -> dict:
    arg_keys = jax.random.split(jax.random.key(seed), 10)
    imagery = draw_imagery(jax.random.fold_in(arg_keys[9], 71), 0)
    stem_weight = normal_values(arg_keys[1], (KDIM, D), KDIM ** -0.5, 0.0546875, ((0, 8), (1, 4)))
    token_gain = jnp.clip(1.0 + 0.18 * jax.random.normal(arg_keys[2], (D,), jnp.float32), 0.099609375, 1.8984375).astype(jnp.bfloat16)
    latents = normal_values(arg_keys[3], (LAT, D), 1.0, 6.0)
    latent_gain = jnp.clip(1.0 + 0.18 * jax.random.normal(arg_keys[4], (D,), jnp.float32), 0.099609375, 1.8984375).astype(jnp.bfloat16)
    query_weight = draw_query_weight(jax.random.fold_in(arg_keys[9], 71), 0)
    key_weight = draw_key_weight(jax.random.fold_in(arg_keys[9], 71), 0)
    value_weight = normal_values(arg_keys[7], (D, D), D ** -0.5, 0.1875, ((0, 8), (1, 4)))
    out_weight = normal_values(arg_keys[8], (D, D), D ** -0.5, 0.1875, ((0, 8), (1, 4)))
    return {"imagery": imagery, "stem_weight": stem_weight, "token_gain": token_gain, "latents": latents, "latent_gain": latent_gain, "query_weight": query_weight, "key_weight": key_weight, "value_weight": value_weight, "out_weight": out_weight}


epsilon = 1e-05

def layer_norm(inputs, gain_row):
    widened = inputs.astype(jnp.float32)
    average = lax.optimization_barrier(jnp.mean(widened, axis=-1, keepdims=True))
    centered = widened - average
    variance = lax.optimization_barrier(jnp.mean(centered * centered, axis=-1, keepdims=True))
    return (centered * lax.rsqrt(variance + epsilon) * gain_row.astype(jnp.float32)).astype(jnp.bfloat16)

def build_patches(strip_rows):
    rim_rows = KER - STRIDE
    padded = jnp.pad(strip_rows, ((0, 0), (0, STRIDE - rim_rows), (0, STRIDE)))
    blocks = padded.reshape(BANDS, TROWS + 1, STRIDE, TCOLS + 1, STRIDE)
    row_cat = jnp.concatenate([blocks[:, :TROWS], blocks[:, 1:, :rim_rows]], axis=2)
    col_cat = jnp.concatenate([row_cat[:, :, :, :TCOLS, :], row_cat[:, :, :, 1:, :rim_rows]], axis=4)
    ordered = jnp.transpose(col_cat, (1, 3, 0, 2, 4))
    return ordered.reshape(TROWS * TCOLS, BANDS * KER * KER)

def reference(imagery, stem_weight, token_gain, latents, latent_gain, query_weight, key_weight, value_weight, out_weight):
    strip_height = STRIDE * TROWS
    strip_count = imagery.shape[1] // strip_height
    extended = jnp.pad(imagery, ((0, 0), (0, KER - STRIDE), (0, 0)))

    def one_strip(strip_index):
        start_row = (strip_index * strip_height).astype(jnp.int32)
        strip_rows = lax.dynamic_slice_in_dim(extended, start_row, strip_height + KER - STRIDE, 1)
        patches = build_patches(strip_rows)
        feature = jnp.dot(patches, stem_weight, preferred_element_type=jnp.float32).astype(jnp.bfloat16)
        token_norm = layer_norm(feature, token_gain)
        keys = jnp.dot(token_norm, key_weight, preferred_element_type=jnp.float32).astype(jnp.bfloat16)
        values = jnp.dot(token_norm, value_weight, preferred_element_type=jnp.float32).astype(jnp.bfloat16)
        return (keys, values)
    keys, values = lax.map(one_strip, jnp.arange(strip_count, dtype=jnp.int32))
    keys = keys.reshape(-1, D)
    values = values.reshape(-1, D)
    latent_norm = layer_norm(latents, latent_gain)
    queries = jnp.dot(latent_norm, query_weight, preferred_element_type=jnp.float32).astype(jnp.bfloat16)
    head_size = D // HEADS
    score_scale = head_size ** (-0.5)
    query_heads = queries.reshape(LAT, HEADS, head_size).transpose(1, 0, 2)
    key_heads = keys.reshape(-1, HEADS, head_size).transpose(1, 0, 2)
    value_heads = values.reshape(-1, HEADS, head_size).transpose(1, 0, 2)

    def one_head(head_items):
        query_block, key_block, value_block = head_items
        scores = jnp.dot(query_block.astype(jnp.float32), key_block.astype(jnp.float32).T) * score_scale
        maxima = lax.optimization_barrier(jnp.max(scores, axis=1, keepdims=True))
        weights = jnp.exp(scores - maxima)
        totals = lax.optimization_barrier(jnp.sum(weights, axis=1, keepdims=True))
        numerator = jnp.dot(weights, value_block.astype(jnp.float32), precision=lax.Precision.HIGHEST)
        return numerator / totals
    attended = lax.map(one_head, (query_heads, key_heads, value_heads))
    mixed = attended.transpose(1, 0, 2).reshape(LAT, D).astype(jnp.bfloat16)
    return jnp.dot(mixed, out_weight.T, preferred_element_type=jnp.float32).astype(jnp.bfloat16)
```

```python
import functools

import jax
import jax.numpy as jnp
from jax import lax
from jax.experimental import pallas as pl
from jax.experimental.pallas import tpu as pltpu
from jax.sharding import PartitionSpec as P

D = 1024
HEADS = 16
LAT = 512
BANDS = 5
KER = 48
STRIDE = 32
TROWS = 2
TCOLS = 32


epsilon = 1e-05


def shifted(block, axis, distance):
    devices = range(lax.axis_size(axis))
    route = [(i - distance, i) for i in devices if i - distance in devices]
    return lax.ppermute(block, axis, route)


def layer_norm(inputs, gain_row):
    widened = inputs.astype(jnp.float32)
    average = jnp.mean(widened, axis=-1, keepdims=True)
    centered = widened - average
    variance = jnp.mean(centered * centered, axis=-1, keepdims=True)
    return (centered * lax.rsqrt(variance + epsilon) * gain_row.astype(jnp.float32)).astype(
        jnp.bfloat16
    )


def build_patches(strip_rows):
    rim_rows = KER - STRIDE
    padded = jnp.pad(strip_rows, ((0, 0), (0, STRIDE - rim_rows), (0, STRIDE)))
    blocks = padded.reshape(BANDS, TROWS + 1, STRIDE, TCOLS + 1, STRIDE)
    row_cat = jnp.concatenate([blocks[:, :TROWS], blocks[:, 1:, :rim_rows]], axis=2)
    col_cat = jnp.concatenate(
        [row_cat[:, :, :, :TCOLS, :], row_cat[:, :, :, 1:, :rim_rows]], axis=4
    )
    ordered = jnp.transpose(col_cat, (1, 3, 0, 2, 4))
    return ordered.reshape(TROWS * TCOLS, BANDS * KER * KER)


def per_device(
    imagery,
    stem_weight,
    token_gain,
    latents,
    latent_gain,
    query_weight,
    key_weight,
    value_weight,
    out_weight,
):
    rim_rows = KER - STRIDE
    below = shifted(imagery[:, :rim_rows, :], "rows", -1)
    patches = build_patches(jnp.concatenate([imagery, below], axis=1))
    token_count = patches.shape[0]
    width_dev = stem_weight.shape[1]
    stem_out = jnp.dot(
        patches,
        lax.all_gather(stem_weight, "rows", axis=0, tiled=True),
        preferred_element_type=jnp.float32,
    )
    feature = lax.all_gather(stem_out.astype(jnp.bfloat16), "heads", axis=1, tiled=True)
    token_norm = layer_norm(feature, token_gain)
    w_query, w_key, w_value, w_out = (
        lax.all_gather(query_weight, "rows", axis=0, tiled=True),
        lax.all_gather(key_weight, "rows", axis=0, tiled=True),
        lax.all_gather(value_weight, "rows", axis=0, tiled=True),
        lax.all_gather(out_weight, "rows", axis=0, tiled=True),
    )
    keys = jnp.dot(token_norm, w_key, preferred_element_type=jnp.float32).astype(jnp.bfloat16)
    values = jnp.dot(token_norm, w_value, preferred_element_type=jnp.float32).astype(jnp.bfloat16)
    head_size = D // HEADS
    heads_dev = width_dev // head_size
    latent_dev = LAT // lax.axis_size("rows")
    first_latent = lax.axis_index("rows") * latent_dev
    queries = jnp.dot(
        layer_norm(latents, latent_gain), w_query, preferred_element_type=jnp.float32
    ).astype(jnp.bfloat16)
    query_split = queries.reshape(LAT, heads_dev, head_size)
    key_split = keys.reshape(token_count, heads_dev, head_size)
    value_split = values.reshape(token_count, heads_dev, head_size)
    scores = jnp.einsum(
        "lhd,thd->lht", query_split, key_split, preferred_element_type=jnp.float32
    ) * head_size ** (-0.5)
    local_peak = jnp.max(scores, axis=2)

    def own_slice(array):
        return lax.dynamic_slice_in_dim(array, first_latent, latent_dev, 0)

    global_peak = lax.pmax(local_peak, "rows")
    weights = jnp.exp(scores - global_peak[:, :, None])
    totals = jnp.sum(weights, axis=2)
    upper_part = weights.astype(jnp.bfloat16)
    lower_part = (weights - upper_part.astype(jnp.float32)).astype(jnp.bfloat16)
    numerator = jnp.einsum(
        "lht,thd->lhd", upper_part, value_split, preferred_element_type=jnp.float32
    )
    numerator = numerator + jnp.einsum(
        "lht,thd->lhd", lower_part, value_split, preferred_element_type=jnp.float32
    )
    totals, numerator = (totals, numerator.reshape(LAT, width_dev))
    totals, numerator = lax.psum((totals, numerator), "rows")
    totals = own_slice(totals)
    numerator = own_slice(numerator)
    attended = numerator.reshape(latent_dev, heads_dev, head_size) / totals[:, :, None]
    mixed = attended.reshape(latent_dev, width_dev).astype(jnp.bfloat16)
    out_terms = lax.dot_general(
        mixed, w_out, (((1,), (1,)), ((), ())), preferred_element_type=jnp.float32
    )
    return lax.psum_scatter(out_terms, "heads", scatter_dimension=1, tiled=True).astype(
        jnp.bfloat16
    )


MESH = pl.DeviceIdType.MESH
VARIANTS = 5
F32 = jnp.float32
BF16 = jnp.bfloat16


def dot(a, b):
    return jnp.dot(a, b, preferred_element_type=F32)


def iota(shape, dim):
    return lax.broadcasted_iota(jnp.int32, shape, dim)


def band_and_line(flat):
    band = jnp.zeros_like(flat)
    for step in range(1, BANDS + 1):
        band = band + (flat >= KER * step).astype(jnp.int32)
    return band, flat - KER * band


def strip_kernel(
    rows,
    heads,
    image_ref,
    stem_ref,
    token_gain_ref,
    latents_ref,
    latent_gain_ref,
    wq_ref,
    wk_ref,
    wv_ref,
    wo_ref,
    out_ref,
    lines_out,
    lines_in,
    wide,
    order,
    ordered,
    stem_sum,
    part_out,
    part_in,
    feature,
    w_first,
    w_second,
    kv,
    out_terms,
    out_in,
    line_s,
    line_r,
    line_fs,
    line_fr,
    part_s,
    part_r,
    feat_s,
    feat_r,
    end_s,
    end_r,
    gz_s,
    gz_r,
    gy_s,
    gy_r,
):
    r = lax.axis_index("rows")
    h = lax.axis_index("heads")
    core = lax.rem(h, 2)
    core_peer = h + 1 - 2 * core
    y_peer = r + 1 - 2 * lax.rem(r, 2)
    per = stem_ref.shape[0] // KER
    pad = lines_in.shape[2]
    width = stem_ref.shape[1]
    pixels = image_ref.shape[2]
    groups = pixels // 128
    started = []

    barrier = pltpu.get_barrier_semaphore()
    for d in range(1, rows):
        pl.semaphore_signal(
            barrier, inc=1, device_id=(lax.rem(r + d, rows), h), device_id_type=MESH
        )
    for d in range(1, heads):
        pl.semaphore_signal(
            barrier, inc=1, device_id=(r, lax.rem(h + d, heads)), device_id_type=MESH
        )

    slots = rows * 2 * pad
    row = iota((slots, 1), 0)
    receiver, second, line = row // (2 * pad), (row // pad) % 2, row % pad
    band, at = band_and_line(per * receiver + line)
    height = image_ref.shape[1]
    source = band * height + jnp.where(second == 1, (at + STRIDE) % height, at)
    pick = (iota((slots, BANDS * height), 1) == source).astype(BF16)
    image = image_ref[...].reshape(BANDS * height, pixels)
    lines_out[...] = dot(pick, image).astype(BF16).reshape(lines_out.shape)
    w_first[r, 0] = wk_ref[...]
    w_first[r, 1] = wv_ref[...]
    w_second[r, 0] = wq_ref[...]
    w_second[r, 1] = wo_ref[...]
    pl.semaphore_wait(barrier, rows - 1 + heads - 1)

    def remote(src, dst, send, recv, to):
        copy = pltpu.make_async_remote_copy(
            src_ref=src,
            dst_ref=dst,
            send_sem=send,
            recv_sem=recv,
            device_id=to,
            device_id_type=MESH,
        )
        copy.start()
        started.append(copy)
        return copy

    def gather_start(buf, which):
        first = [
            remote(
                buf.at[r],
                buf.at[r],
                gz_s.at[which, d],
                gz_r.at[which, d],
                (lax.rem(r + 2 * d, rows), h),
            )
            for d in range(1, rows // 2)
        ]
        across = remote(
            buf.at[r], buf.at[r], gy_s.at[which, 0], gy_r.at[which, 0], (y_peer, h)
        )
        return first, [across]

    def gather_forward(buf, which, state):
        first, across = state
        for d, copy in enumerate(first, 1):
            copy.wait_recv()
            slot = lax.rem(r + rows - 2 * d, rows)
            across.append(
                remote(
                    buf.at[slot],
                    buf.at[slot],
                    gy_s.at[which, d],
                    gy_r.at[which, d],
                    (y_peer, h),
                )
            )

    def gather_wait(state):
        for copy in state[1]:
            copy.wait_recv()

    line_copies = []
    for d in range(1, rows):
        to = lax.rem(r + d, rows)
        line_copies.append(
            remote(
                lines_out.at[to, core],
                lines_in.at[r, core],
                line_s.at[d],
                line_r.at[d],
                (to, h),
            )
        )
    first_state = gather_start(w_first, 0)
    second_state = gather_start(w_second, 1)
    lines_in[r] = lines_out[r]

    wide[...] = jnp.zeros_like(wide)

    def widen(f, carry):
        block = stem_ref[pl.ds(pl.multiple_of(f * KER, 16), KER), :]
        for v in range(VARIANTS - 2):
            wide[
                pl.ds(pl.multiple_of(f * 128 + STRIDE * v, 16), KER),
                v * width : (v + 1) * width,
            ] = block
        v = VARIANTS - 2
        wide[
            pl.ds(pl.multiple_of(f * 128 + STRIDE * v, 16), STRIDE),
            v * width : (v + 1) * width,
        ] = block[:STRIDE]
        v = VARIANTS - 1
        wide[
            pl.ds(pl.multiple_of(f * 128, 16), KER - STRIDE), v * width : (v + 1) * width
        ] = block[STRIDE:]
        return carry

    lax.fori_loop(0, per, widen, 0)

    token_rows = rows * TROWS
    row = iota((per * token_rows, 1), 0)
    line, token_row = row // token_rows, row % token_rows
    _, at = band_and_line(per * r + line)
    odd = token_row % 2
    strip = token_row // 2 + jnp.where((odd == 1) & (at >= STRIDE), 1, 0)
    target = (strip * 2 + odd) * pad + line
    order[...] = (iota(order.shape, 1) == target).astype(BF16)

    forwards = []
    for d, copy in enumerate(line_copies, 1):
        copy.wait_recv()
        slot = lax.rem(r + rows - d, rows)
        forwards.append(
            remote(
                lines_in.at[slot, core],
                lines_in.at[slot, core],
                line_fs.at[d],
                line_fr.at[d],
                (r, core_peer),
            )
        )
    for copy in forwards:
        copy.wait_recv()
    ordered[...] = dot(order[...], lines_in[...].reshape(slots, pixels)).astype(BF16)

    at_once = 6
    stem_sum[...] = jnp.zeros_like(stem_sum)

    def stem_step(step, carry):
        blocks = []
        for k in range(at_once):
            f = step * at_once + k
            x = ordered[pl.ds(pl.multiple_of(f * token_rows, 16), token_rows), :]
            blocks.append(
                jnp.concatenate([x[:, 128 * g : 128 * g + 128] for g in range(groups)], axis=0)
            )
        left = jnp.concatenate(blocks, axis=1)
        depth = at_once * 128
        stem_sum[...] += dot(left, wide[pl.ds(pl.multiple_of(step * depth, 128), depth), :])
        return carry

    lax.fori_loop(0, per // at_once, stem_step, 0)
    last = VARIANTS - 2
    rim = jnp.concatenate(
        [
            stem_sum[token_rows:, (last + 1) * width :],
            jnp.zeros((token_rows, width), F32),
        ],
        axis=0,
    )
    sums = jnp.concatenate(
        [
            stem_sum[:, : last * width],
            stem_sum[:, last * width : (last + 1) * width] + rim,
        ],
        axis=1,
    ).astype(BF16)
    each = groups * TROWS
    row = iota((rows * each, 1), 0)
    strip, group, inner = row // each, (row % each) // TROWS, row % TROWS
    turn = iota((rows * each, rows * each), 1) == group * token_rows + strip * TROWS + inner
    part_out[...] = dot(turn.astype(BF16), sums).astype(BF16).reshape(part_out.shape)

    part_copies = []
    for d in range(1, rows):
        to = lax.rem(r + d, rows)
        part_copies.append(
            remote(part_out.at[to], part_in.at[r], part_s.at[d], part_r.at[d], (to, h))
        )
    part_in[r] = part_out[r]

    def norm(x, gain_ref):
        average = jnp.mean(x, axis=-1, keepdims=True)
        centered = x - average
        variance = jnp.mean(centered * centered, axis=-1, keepdims=True)
        return (centered * lax.rsqrt(variance + epsilon) * gain_ref[...].astype(F32)).astype(BF16)

    own = latents_ref.shape[0] // rows
    latent_norm = norm(
        latents_ref[pl.ds(pl.multiple_of(r * own, own), own), :].astype(F32), latent_gain_ref
    )
    gather_forward(w_first, 0, first_state)
    for copy in part_copies:
        copy.wait_recv()
    total = jnp.sum(part_in[...].astype(F32), axis=0)
    feature[h] = jnp.concatenate(
        [total[:, v * width : (v + 1) * width] for v in range(last + 1)], axis=0
    ).astype(BF16)

    feat_copies = []
    for d in range(1, heads):
        feat_copies.append(
            remote(
                feature.at[h],
                feature.at[h],
                feat_s.at[d],
                feat_r.at[d],
                (r, lax.rem(h + d, heads)),
            )
        )
    gather_wait(first_state)
    for copy in feat_copies:
        copy.wait_recv()
    token_norm = norm(
        jnp.concatenate([feature[k] for k in range(heads)], axis=1).astype(F32), token_gain_ref
    )
    for k in range(2):
        kv[r, k] = dot(token_norm, w_first[:, k].reshape(D, width)).astype(BF16)
    kv_state = gather_start(kv, 2)

    gather_forward(w_second, 1, second_state)
    gather_forward(kv, 2, kv_state)
    gather_wait(second_state)
    queries = dot(latent_norm, w_second[:, 0].reshape(D, width)).astype(BF16)
    gather_wait(kv_state)

    tokens = kv.shape[0] * kv.shape[2]
    keys = kv[:, 0].reshape(tokens, width)
    values = kv[:, 1].reshape(tokens, width)
    size = D // HEADS
    mixed = []
    for pair in range(width // 128):
        cols = slice(128 * pair, 128 * pair + 128)
        q, k, v = queries[:, cols], keys[:, cols], values[:, cols]
        side = iota((own, 128), 1) < size
        halves = []
        for low in (True, False):
            keep = side if low else jnp.logical_not(side)
            mine = jnp.where(keep, q.astype(F32), 0.0).astype(BF16)
            scores = lax.dot_general(
                mine, k, (((1,), (1,)), ((), ())), preferred_element_type=F32
            ) * size ** (-0.5)
            weights = jnp.exp(scores - jnp.max(scores, axis=1, keepdims=True))
            totals = jnp.sum(weights, axis=1, keepdims=True)
            upper = weights.astype(BF16)
            lower = (weights - upper.astype(F32)).astype(BF16)
            halves.append((dot(upper, v) + dot(lower, v)) / totals)
        mixed.append(jnp.where(side, halves[0], halves[1]).astype(BF16))
    mixed = jnp.concatenate(mixed, axis=1)

    for k in range(heads):
        per_head = w_second.shape[0] // heads
        block = w_second[per_head * k : per_head * (k + 1), 1].reshape(width, width)
        out_terms[k] = lax.dot_general(
            mixed, block, (((1,), (1,)), ((), ())), preferred_element_type=F32
        )
    end_copies = []
    for d in range(1, heads):
        to = lax.rem(h + d, heads)
        end_copies.append(
            remote(out_terms.at[to], out_in.at[d - 1], end_s.at[d], end_r.at[d], (r, to))
        )
    result = out_terms[h]
    for d, copy in enumerate(end_copies, 1):
        copy.wait_recv()
        result = result + out_in[d - 1]
    out_ref[...] = result.astype(BF16)
    for copy in started:
        copy.wait_send()


def fused(rows, heads):
    def per_chip(imagery, stem, token_gain, latents, latent_gain, wq, wk, wv, wo):
        per = stem.shape[0] // KER
        pad = -(-per // 16) * 16
        width = stem.shape[1]
        pixels = imagery.shape[2]
        groups = pixels // 128
        own = latents.shape[0] // rows
        tokens = TROWS * TCOLS
        token_rows = rows * TROWS
        dma = pltpu.SemaphoreType.DMA
        return pl.pallas_call(
            functools.partial(strip_kernel, rows, heads),
            out_shape=jax.ShapeDtypeStruct((own, width), BF16),
            in_specs=[pl.BlockSpec(memory_space=pltpu.VMEM)] * 9,
            out_specs=pl.BlockSpec(memory_space=pltpu.VMEM),
            scratch_shapes=[
                pltpu.VMEM((rows, 2, pad, pixels), BF16),
                pltpu.VMEM((rows, 2, pad, pixels), BF16),
                pltpu.VMEM((per * 128, VARIANTS * width), BF16),
                pltpu.VMEM((per * token_rows, rows * 2 * pad), BF16),
                pltpu.VMEM((per * token_rows, pixels), BF16),
                pltpu.VMEM((groups * token_rows, VARIANTS * width), F32),
                pltpu.VMEM((rows, groups * TROWS, 4 * width), BF16),
                pltpu.VMEM((rows, groups * TROWS, 4 * width), BF16),
                pltpu.VMEM((heads, tokens, width), BF16),
                pltpu.VMEM((rows, 2, wk.shape[0], width), BF16),
                pltpu.VMEM((rows, 2, wk.shape[0], width), BF16),
                pltpu.VMEM((rows, 2, tokens, width), BF16),
                pltpu.VMEM((heads, own, width), F32),
                pltpu.VMEM((heads - 1, own, width), F32),
                dma((rows,)),
                dma((rows,)),
                dma((rows,)),
                dma((rows,)),
                dma((rows,)),
                dma((rows,)),
                dma((heads,)),
                dma((heads,)),
                dma((heads,)),
                dma((heads,)),
                dma((3, rows // 2)),
                dma((3, rows // 2)),
                dma((3, rows // 2)),
                dma((3, rows // 2)),
            ],
            compiler_params=pltpu.CompilerParams(
                collective_id=0, has_side_effects=True, vmem_limit_bytes=48 * 2**20
            ),
        )(
            imagery,
            stem,
            token_gain.reshape(1, -1),
            latents,
            latent_gain.reshape(1, -1),
            wq,
            wk,
            wv,
            wo,
        )

    return per_chip


def lines_fit(mesh):
    rows = mesh.shape["rows"]
    return BANDS * KER % rows == 0 and rows <= 8


def solution(mesh):
    body = fused(mesh.shape["rows"], mesh.shape["heads"]) if lines_fit(mesh) else per_device
    return jax.shard_map(
        body,
        mesh=mesh,
        in_specs=(
            P(None, "rows", None),
            P("rows", "heads"),
            P(),
            P(),
            P(),
            P("rows", "heads"),
            P("rows", "heads"),
            P("rows", "heads"),
            P("rows", "heads"),
        ),
        out_specs=P("rows", "heads"),
        check_vma=False,
    )
```

```python
import functools

import jax
import jax.numpy as jnp
from jax import lax
from jax.experimental import pallas as pl
from jax.experimental.pallas import tpu as pltpu
from jax.sharding import PartitionSpec as P

D = 1024
HEADS = 16
LAT = 512
BANDS = 5
KER = 48
STRIDE = 32
TROWS = 2
TCOLS = 32


epsilon = 1e-05


def shifted(block, axis, distance):
    devices = range(lax.axis_size(axis))
    route = [(i - distance, i) for i in devices if i - distance in devices]
    return lax.ppermute(block, axis, route)


def layer_norm(inputs, gain_row):
    widened = inputs.astype(jnp.float32)
    average = jnp.mean(widened, axis=-1, keepdims=True)
    centered = widened - average
    variance = jnp.mean(centered * centered, axis=-1, keepdims=True)
    return (centered * lax.rsqrt(variance + epsilon) * gain_row.astype(jnp.float32)).astype(
        jnp.bfloat16
    )


def build_patches(strip_rows):
    rim_rows = KER - STRIDE
    padded = jnp.pad(strip_rows, ((0, 0), (0, STRIDE - rim_rows), (0, STRIDE)))
    blocks = padded.reshape(BANDS, TROWS + 1, STRIDE, TCOLS + 1, STRIDE)
    row_cat = jnp.concatenate([blocks[:, :TROWS], blocks[:, 1:, :rim_rows]], axis=2)
    col_cat = jnp.concatenate(
        [row_cat[:, :, :, :TCOLS, :], row_cat[:, :, :, 1:, :rim_rows]], axis=4
    )
    ordered = jnp.transpose(col_cat, (1, 3, 0, 2, 4))
    return ordered.reshape(TROWS * TCOLS, BANDS * KER * KER)


def per_device(
    imagery,
    stem_weight,
    token_gain,
    latents,
    latent_gain,
    query_weight,
    key_weight,
    value_weight,
    out_weight,
):
    rim_rows = KER - STRIDE
    below = shifted(imagery[:, :rim_rows, :], "rows", -1)
    patches = build_patches(jnp.concatenate([imagery, below], axis=1))
    token_count = patches.shape[0]
    width_dev = stem_weight.shape[1]
    stem_out = jnp.dot(
        patches,
        lax.all_gather(stem_weight, "rows", axis=0, tiled=True),
        preferred_element_type=jnp.float32,
    )
    feature = lax.all_gather(stem_out.astype(jnp.bfloat16), "heads", axis=1, tiled=True)
    token_norm = layer_norm(feature, token_gain)
    w_query, w_key, w_value, w_out = (
        lax.all_gather(query_weight, "rows", axis=0, tiled=True),
        lax.all_gather(key_weight, "rows", axis=0, tiled=True),
        lax.all_gather(value_weight, "rows", axis=0, tiled=True),
        lax.all_gather(out_weight, "rows", axis=0, tiled=True),
    )
    keys = jnp.dot(token_norm, w_key, preferred_element_type=jnp.float32).astype(jnp.bfloat16)
    values = jnp.dot(token_norm, w_value, preferred_element_type=jnp.float32).astype(jnp.bfloat16)
    head_size = D // HEADS
    heads_dev = width_dev // head_size
    latent_dev = LAT // lax.axis_size("rows")
    first_latent = lax.axis_index("rows") * latent_dev
    queries = jnp.dot(
        layer_norm(latents, latent_gain), w_query, preferred_element_type=jnp.float32
    ).astype(jnp.bfloat16)
    query_split = queries.reshape(LAT, heads_dev, head_size)
    key_split = keys.reshape(token_count, heads_dev, head_size)
    value_split = values.reshape(token_count, heads_dev, head_size)
    scores = jnp.einsum(
        "lhd,thd->lht", query_split, key_split, preferred_element_type=jnp.float32
    ) * head_size ** (-0.5)
    local_peak = jnp.max(scores, axis=2)

    def own_slice(array):
        return lax.dynamic_slice_in_dim(array, first_latent, latent_dev, 0)

    global_peak = lax.pmax(local_peak, "rows")
    weights = jnp.exp(scores - global_peak[:, :, None])
    totals = jnp.sum(weights, axis=2)
    upper_part = weights.astype(jnp.bfloat16)
    lower_part = (weights - upper_part.astype(jnp.float32)).astype(jnp.bfloat16)
    numerator = jnp.einsum(
        "lht,thd->lhd", upper_part, value_split, preferred_element_type=jnp.float32
    )
    numerator = numerator + jnp.einsum(
        "lht,thd->lhd", lower_part, value_split, preferred_element_type=jnp.float32
    )
    totals, numerator = (totals, numerator.reshape(LAT, width_dev))
    totals, numerator = lax.psum((totals, numerator), "rows")
    totals = own_slice(totals)
    numerator = own_slice(numerator)
    attended = numerator.reshape(latent_dev, heads_dev, head_size) / totals[:, :, None]
    mixed = attended.reshape(latent_dev, width_dev).astype(jnp.bfloat16)
    out_terms = lax.dot_general(
        mixed, w_out, (((1,), (1,)), ((), ())), preferred_element_type=jnp.float32
    )
    return lax.psum_scatter(out_terms, "heads", scatter_dimension=1, tiled=True).astype(
        jnp.bfloat16
    )


MESH = pl.DeviceIdType.MESH
VARIANTS = 5
F32 = jnp.float32
BF16 = jnp.bfloat16


def dot(a, b):
    return jnp.dot(a, b, preferred_element_type=F32)


def iota(shape, dim):
    return lax.broadcasted_iota(jnp.int32, shape, dim)


def band_and_line(flat):
    band = jnp.zeros_like(flat)
    for step in range(1, BANDS + 1):
        band = band + (flat >= KER * step).astype(jnp.int32)
    return band, flat - KER * band


def strip_kernel(
    rows,
    heads,
    image_ref,
    stem_ref,
    token_gain_ref,
    latents_ref,
    latent_gain_ref,
    wq_ref,
    wk_ref,
    wv_ref,
    wo_ref,
    out_ref,
    image,
    stem,
    latent_rows,
    latent_norm,
    query_part,
    query_in,
    lines_out,
    lines_in,
    wide,
    order,
    ordered,
    stem_sum,
    part_out,
    part_in,
    feature,
    w_first,
    w_second,
    kv,
    out_terms,
    out_in,
    local,
    line_s,
    line_r,
    query_s,
    query_r,
    part_s,
    part_r,
    feat_s,
    feat_r,
    end_s,
    end_r,
    z_s,
    z_r,
    gz_s,
    gz_r,
    gy_s,
    gy_r,
):
    r = lax.axis_index("rows")
    h = lax.axis_index("heads")
    core = lax.rem(h, 2)
    core_peer = h + 1 - 2 * core
    half = h // 2
    x_peer = lax.rem(h + 2, heads)
    y = lax.rem(r, 2)
    z = r // 2
    y_peer = r + 1 - 2 * y
    z_opposite = lax.rem(r + 4, rows)
    z_pair = r + 2 - 4 * lax.rem(z, 2)
    z_last = lax.rem(z_pair + 4, rows)
    own = latents_ref.shape[0] // rows
    per = stem_ref.shape[0] // KER
    pad = lines_in.shape[2]
    width = stem_ref.shape[1]
    pixels = image_ref.shape[2]
    groups = pixels // 128
    started = []

    loads = [
        pltpu.make_async_copy(source, target, local.at[k])
        for k, (source, target) in enumerate(
            [
                (image_ref, image),
                (wk_ref, w_first.at[r, 0]),
                (wv_ref, w_first.at[r, 1]),
                (stem_ref, stem),
                (wq_ref, w_second.at[r, 0]),
                (wo_ref, w_second.at[r, 1]),
                (
                    latents_ref.at[pl.ds(pl.multiple_of(z * 2 * own, 2 * own), 2 * own)],
                    latent_rows,
                ),
            ]
        )
    ]
    for copy in loads:
        copy.start()

    barrier = pltpu.get_barrier_semaphore()
    for d in range(1, rows):
        pl.semaphore_signal(
            barrier, inc=1, device_id=(lax.rem(r + d, rows), h), device_id_type=MESH
        )
    for d in range(1, heads):
        pl.semaphore_signal(
            barrier, inc=1, device_id=(r, lax.rem(h + d, heads)), device_id_type=MESH
        )

    slots = rows * 2 * pad
    row = iota((slots, 1), 0)
    receiver, second, line = row // (2 * pad), (row // pad) % 2, row % pad
    band, at = band_and_line(per * receiver + line)
    height = image_ref.shape[1]
    source = band * height + jnp.where(second == 1, (at + STRIDE) % height, at)
    pick = (iota((slots, BANDS * height), 1) == source).astype(BF16)
    loads[0].wait()
    flat = image[...].reshape(BANDS * height, pixels)
    lines_out[...] = dot(pick, flat).astype(BF16).reshape(lines_out.shape)
    pl.semaphore_wait(barrier, rows - 1 + heads - 1)

    def remote(src, dst, send, recv, to):
        copy = pltpu.make_async_remote_copy(
            src_ref=src,
            dst_ref=dst,
            send_sem=send,
            recv_sem=recv,
            device_id=to,
            device_id_type=MESH,
        )
        copy.start()
        started.append(copy)
        return copy

    def gather_start(buf, which):
        first = [
            remote(
                buf.at[r],
                buf.at[r],
                gz_s.at[d],
                gz_r.at[d],
                (lax.rem(r + 2 * d, rows), h),
            )
            for d in range(1, rows // 2)
        ]
        across = remote(
            buf.at[r], buf.at[r], gy_s.at[which, 0], gy_r.at[which, 0], (y_peer, h)
        )
        return first, [across]

    def gather_forward(buf, which, state):
        first, across = state
        for d, copy in enumerate(first, 1):
            copy.wait_recv()
            slot = lax.rem(r + rows - 2 * d, rows)
            across.append(
                remote(
                    buf.at[slot],
                    buf.at[slot],
                    gy_s.at[which, d],
                    gy_r.at[which, d],
                    (y_peer, h),
                )
            )

    def gather_wait(state):
        for copy in state[1]:
            copy.wait_recv()

    def z_start(buf, which, part):
        return [
            remote(buf.at[r], buf.at[r], z_s.at[which, 0], z_r.at[which, 0], (z_opposite, h)),
            remote(buf.at[r], buf.at[r], z_s.at[which, 1], z_r.at[which, 1], (z_pair, h)),
        ], [y_send(part(buf, r), which, 0)]

    def y_send(ref, which, k):
        return remote(ref, ref, gy_s.at[which, k], gy_r.at[which, k], (y_peer, h))

    def z_pass(buf, which, part, state):
        first, across = state
        first[0].wait_recv()
        ref = buf.at[z_opposite]
        first.append(remote(ref, ref, z_s.at[which, 2], z_r.at[which, 2], (z_pair, h)))
        across.append(y_send(part(buf, z_opposite), which, 1))
        first[1].wait_recv()
        across.append(y_send(part(buf, z_pair), which, 2))

    def z_end(buf, which, part, state):
        first, across = state
        first[2].wait_recv()
        across.append(y_send(part(buf, z_last), which, 3))

    def whole_slot(buf, slot):
        return buf.at[slot]

    def second_only(buf, slot):
        return buf.at[slot, 1]

    quarter = pad // 2

    def lines_at(ref, slot, part):
        return ref.at[slot, core, pl.ds(pl.multiple_of(part * quarter, quarter), quarter)]

    line_copies = []
    for d in range(1, rows):
        to = lax.rem(r + d, rows)
        line_copies.append(
            remote(
                lines_at(lines_out, to, half),
                lines_at(lines_in, r, half),
                line_s.at[0, d],
                line_r.at[0, d],
                (to, h),
            )
        )
    lines_in[r] = lines_out[r]
    loads[1].wait()
    loads[2].wait()

    wide[...] = jnp.zeros_like(wide)
    first_state = z_start(w_first, 0, whole_slot)
    loads[3].wait()

    def widen(f, carry):
        block = stem[pl.ds(pl.multiple_of(f * KER, 16), KER), :]
        for v in range(VARIANTS - 2):
            wide[
                pl.ds(pl.multiple_of(f * 128 + STRIDE * v, 16), KER),
                v * width : (v + 1) * width,
            ] = block
        v = VARIANTS - 2
        wide[
            pl.ds(pl.multiple_of(f * 128 + STRIDE * v, 16), STRIDE),
            v * width : (v + 1) * width,
        ] = block[:STRIDE]
        v = VARIANTS - 1
        wide[
            pl.ds(pl.multiple_of(f * 128, 16), KER - STRIDE), v * width : (v + 1) * width
        ] = block[STRIDE:]
        return carry

    lax.fori_loop(0, per, widen, 0)

    token_rows = rows * TROWS
    row = iota((per * token_rows, 1), 0)
    line, token_row = row // token_rows, row % token_rows
    _, at = band_and_line(per * r + line)
    odd = token_row % 2
    strip = token_row // 2 + jnp.where((odd == 1) & (at >= STRIDE), 1, 0)
    target = (strip * 2 + odd) * pad + line
    order[...] = (iota(order.shape, 1) == target).astype(BF16)

    def pass_line(slot, part, k, d, to):
        ref = lines_at(lines_in, slot, part)
        return remote(ref, ref, line_s.at[k, d], line_r.at[k, d], (r, to))

    over_x, over_core = [], []
    for d, copy in enumerate(line_copies, 1):
        copy.wait_recv()
        slot = lax.rem(r + rows - d, rows)
        over_x.append(pass_line(slot, half, 1, d, x_peer))
        over_core.append(pass_line(slot, half, 2, d, core_peer))
    for d, copy in enumerate(over_x, 1):
        copy.wait_recv()
        slot = lax.rem(r + rows - d, rows)
        over_core.append(pass_line(slot, 1 - half, 3, d, core_peer))
    loads[4].wait()
    loads[5].wait()
    second_state = z_start(w_second, 1, second_only)
    for copy in over_core:
        copy.wait_recv()
    ordered[...] = dot(order[...], lines_in[...].reshape(slots, pixels)).astype(BF16)

    z_pass(w_first, 0, whole_slot, first_state)

    at_once = 6
    stem_sum[...] = jnp.zeros_like(stem_sum)

    def stem_step(step, carry):
        blocks = []
        for k in range(at_once):
            f = step * at_once + k
            x = ordered[pl.ds(pl.multiple_of(f * token_rows, 16), token_rows), :]
            blocks.append(
                jnp.concatenate([x[:, 128 * g : 128 * g + 128] for g in range(groups)], axis=0)
            )
        left = jnp.concatenate(blocks, axis=1)
        depth = at_once * 128
        stem_sum[...] += dot(left, wide[pl.ds(pl.multiple_of(step * depth, 128), depth), :])
        return carry

    lax.fori_loop(0, per // at_once, stem_step, 0)
    last = VARIANTS - 2
    rim = jnp.concatenate(
        [
            stem_sum[token_rows:, (last + 1) * width :],
            jnp.zeros((token_rows, width), F32),
        ],
        axis=0,
    )
    sums = jnp.concatenate(
        [
            stem_sum[:, : last * width],
            stem_sum[:, last * width : (last + 1) * width] + rim,
        ],
        axis=1,
    ).astype(BF16)
    each = groups * TROWS
    row = iota((rows * each, 1), 0)
    strip, group, inner = row // each, (row % each) // TROWS, row % TROWS
    turn = iota((rows * each, rows * each), 1) == group * token_rows + strip * TROWS + inner
    part_out[...] = dot(turn.astype(BF16), sums).astype(BF16).reshape(part_out.shape)

    part_copies = []
    for d in range(1, rows):
        to = lax.rem(r + d, rows)
        part_copies.append(
            remote(part_out.at[to], part_in.at[r], part_s.at[d], part_r.at[d], (to, h))
        )
    part_in[r] = part_out[r]

    def norm(x, gain_ref):
        average = jnp.mean(x, axis=-1, keepdims=True)
        centered = x - average
        variance = jnp.mean(centered * centered, axis=-1, keepdims=True)
        return (centered * lax.rsqrt(variance + epsilon) * gain_ref[...].astype(F32)).astype(BF16)

    z_end(w_first, 0, whole_slot, first_state)
    loads[6].wait()
    latent_norm[...] = norm(latent_rows[...].astype(F32), latent_gain_ref)
    for copy in part_copies:
        copy.wait_recv()
    total = jnp.sum(part_in[...].astype(F32), axis=0)
    feature[h] = jnp.concatenate(
        [total[:, v * width : (v + 1) * width] for v in range(last + 1)], axis=0
    ).astype(BF16)

    feat_copies = []
    for d in range(1, heads):
        feat_copies.append(
            remote(
                feature.at[h],
                feature.at[h],
                feat_s.at[d],
                feat_r.at[d],
                (r, lax.rem(h + d, heads)),
            )
        )
    z_pass(w_second, 1, second_only, second_state)
    gather_wait(first_state)
    for copy in feat_copies:
        copy.wait_recv()
    token_norm = norm(
        jnp.concatenate([feature[k] for k in range(heads)], axis=1).astype(F32), token_gain_ref
    )
    for k in range(2):
        kv[r, k] = dot(token_norm, w_first[:, k].reshape(D, width)).astype(BF16)
    kv_state = gather_start(kv, 2)

    z_end(w_second, 1, second_only, second_state)
    depth = wq_ref.shape[0]
    part = jnp.zeros((2 * own, width), F32)
    for k in range(rows // 2):
        at = 2 * k + y
        part = part + dot(
            latent_norm[:, pl.ds(pl.multiple_of(at * depth, depth), depth)], w_second[at, 0]
        )
    query_part[...] = part.reshape(query_part.shape)
    query_copy = remote(query_part.at[1 - y], query_in, query_s, query_r, (y_peer, h))
    gather_forward(kv, 2, kv_state)
    query_copy.wait_recv()
    queries = (query_part[y] + query_in[...]).astype(BF16)
    gather_wait(kv_state)

    tokens = kv.shape[0] * kv.shape[2]
    keys = kv[:, 0].reshape(tokens, width)
    values = kv[:, 1].reshape(tokens, width)
    size = D // HEADS
    mixed = []
    for pair in range(width // 128):
        cols = slice(128 * pair, 128 * pair + 128)
        q, k, v = queries[:, cols], keys[:, cols], values[:, cols]
        side = iota((own, 128), 1) < size
        halves = []
        for low in (True, False):
            keep = side if low else jnp.logical_not(side)
            mine = jnp.where(keep, q.astype(F32), 0.0).astype(BF16)
            scores = lax.dot_general(
                mine, k, (((1,), (1,)), ((), ())), preferred_element_type=F32
            ) * size ** (-0.5)
            weights = jnp.exp(scores - jnp.max(scores, axis=1, keepdims=True))
            totals = jnp.sum(weights, axis=1, keepdims=True)
            upper = weights.astype(BF16)
            lower = (weights - upper.astype(F32)).astype(BF16)
            halves.append((dot(upper, v) + dot(lower, v)) / totals)
        mixed.append(jnp.where(side, halves[0], halves[1]).astype(BF16))
    mixed = jnp.concatenate(mixed, axis=1)

    gather_wait(second_state)
    for k in range(heads):
        per_head = w_second.shape[0] // heads
        block = w_second[per_head * k : per_head * (k + 1), 1].reshape(width, width)
        out_terms[k] = lax.dot_general(
            mixed, block, (((1,), (1,)), ((), ())), preferred_element_type=F32
        )
    end_copies = []
    for d in range(1, heads):
        to = lax.rem(h + d, heads)
        end_copies.append(
            remote(out_terms.at[to], out_in.at[d - 1], end_s.at[d], end_r.at[d], (r, to))
        )
    result = out_terms[h]
    for d, copy in enumerate(end_copies, 1):
        copy.wait_recv()
        result = result + out_in[d - 1]
    out_ref[...] = result.astype(BF16)
    for copy in started:
        copy.wait_send()


def fused(rows, heads):
    def per_chip(imagery, stem, token_gain, latents, latent_gain, wq, wk, wv, wo):
        per = stem.shape[0] // KER
        pad = -(-per // 16) * 16
        width = stem.shape[1]
        pixels = imagery.shape[2]
        groups = pixels // 128
        own = latents.shape[0] // rows
        tokens = TROWS * TCOLS
        token_rows = rows * TROWS
        dma = pltpu.SemaphoreType.DMA
        return pl.pallas_call(
            functools.partial(strip_kernel, rows, heads),
            out_shape=jax.ShapeDtypeStruct((own, width), BF16),
            in_specs=[
                pl.BlockSpec(memory_space=pltpu.VMEM if k in (2, 4) else pltpu.HBM)
                for k in range(9)
            ],
            out_specs=pl.BlockSpec(memory_space=pltpu.VMEM),
            scratch_shapes=[
                pltpu.VMEM(imagery.shape, BF16),
                pltpu.VMEM(stem.shape, BF16),
                pltpu.VMEM((2 * own, D), BF16),
                pltpu.VMEM((2 * own, D), BF16),
                pltpu.VMEM((2, own, width), F32),
                pltpu.VMEM((own, width), F32),
                pltpu.VMEM((rows, 2, pad, pixels), BF16),
                pltpu.VMEM((rows, 2, pad, pixels), BF16),
                pltpu.VMEM((per * 128, VARIANTS * width), BF16),
                pltpu.VMEM((per * token_rows, rows * 2 * pad), BF16),
                pltpu.VMEM((per * token_rows, pixels), BF16),
                pltpu.VMEM((groups * token_rows, VARIANTS * width), F32),
                pltpu.VMEM((rows, groups * TROWS, 4 * width), BF16),
                pltpu.VMEM((rows, groups * TROWS, 4 * width), BF16),
                pltpu.VMEM((heads, tokens, width), BF16),
                pltpu.VMEM((rows, 2, wk.shape[0], width), BF16),
                pltpu.VMEM((rows, 2, wk.shape[0], width), BF16),
                pltpu.VMEM((rows, 2, tokens, width), BF16),
                pltpu.VMEM((heads, own, width), F32),
                pltpu.VMEM((heads - 1, own, width), F32),
                dma((7,)),
                dma((4, rows)),
                dma((4, rows)),
                dma,
                dma,
                dma((rows,)),
                dma((rows,)),
                dma((heads,)),
                dma((heads,)),
                dma((heads,)),
                dma((heads,)),
                dma((2, 3)),
                dma((2, 3)),
                dma((rows // 2,)),
                dma((rows // 2,)),
                dma((3, rows // 2)),
                dma((3, rows // 2)),
            ],
            compiler_params=pltpu.CompilerParams(
                collective_id=0, has_side_effects=True, vmem_limit_bytes=48 * 2**20
            ),
        )(
            imagery,
            stem,
            token_gain.reshape(1, -1),
            latents,
            latent_gain.reshape(1, -1),
            wq,
            wk,
            wv,
            wo,
        )

    return per_chip


def lines_fit(mesh):
    return mesh.shape["rows"] == 8 and mesh.shape["heads"] == 4


def solution(mesh):
    body = fused(mesh.shape["rows"], mesh.shape["heads"]) if lines_fit(mesh) else per_device
    return jax.shard_map(
        body,
        mesh=mesh,
        in_specs=(
            P(None, "rows", None),
            P("rows", "heads"),
            P(),
            P(),
            P(),
            P("rows", "heads"),
            P("rows", "heads"),
            P("rows", "heads"),
            P("rows", "heads"),
        ),
        out_specs=P("rows", "heads"),
        check_vma=False,
    )
```

```python
import functools

import jax
import jax.numpy as jnp
from jax import lax
from jax.experimental import pallas as pl
from jax.experimental.pallas import tpu as pltpu
from jax.sharding import PartitionSpec as P

D = 1024
HEADS = 16
LAT = 512
BANDS = 5
KER = 48
STRIDE = 32
TROWS = 2
TCOLS = 32


epsilon = 1e-05


def shifted(block, axis, distance):
    devices = range(lax.axis_size(axis))
    route = [(i - distance, i) for i in devices if i - distance in devices]
    return lax.ppermute(block, axis, route)


def layer_norm(inputs, gain_row):
    widened = inputs.astype(jnp.float32)
    average = jnp.mean(widened, axis=-1, keepdims=True)
    centered = widened - average
    variance = jnp.mean(centered * centered, axis=-1, keepdims=True)
    return (centered * lax.rsqrt(variance + epsilon) * gain_row.astype(jnp.float32)).astype(
        jnp.bfloat16
    )


def build_patches(strip_rows):
    rim_rows = KER - STRIDE
    padded = jnp.pad(strip_rows, ((0, 0), (0, STRIDE - rim_rows), (0, STRIDE)))
    blocks = padded.reshape(BANDS, TROWS + 1, STRIDE, TCOLS + 1, STRIDE)
    row_cat = jnp.concatenate([blocks[:, :TROWS], blocks[:, 1:, :rim_rows]], axis=2)
    col_cat = jnp.concatenate(
        [row_cat[:, :, :, :TCOLS, :], row_cat[:, :, :, 1:, :rim_rows]], axis=4
    )
    ordered = jnp.transpose(col_cat, (1, 3, 0, 2, 4))
    return ordered.reshape(TROWS * TCOLS, BANDS * KER * KER)


def per_device(
    imagery,
    stem_weight,
    token_gain,
    latents,
    latent_gain,
    query_weight,
    key_weight,
    value_weight,
    out_weight,
):
    rim_rows = KER - STRIDE
    below = shifted(imagery[:, :rim_rows, :], "rows", -1)
    patches = build_patches(jnp.concatenate([imagery, below], axis=1))
    token_count = patches.shape[0]
    width_dev = stem_weight.shape[1]
    stem_out = jnp.dot(
        patches,
        lax.all_gather(stem_weight, "rows", axis=0, tiled=True),
        preferred_element_type=jnp.float32,
    )
    feature = lax.all_gather(stem_out.astype(jnp.bfloat16), "heads", axis=1, tiled=True)
    token_norm = layer_norm(feature, token_gain)
    w_query, w_key, w_value, w_out = (
        lax.all_gather(query_weight, "rows", axis=0, tiled=True),
        lax.all_gather(key_weight, "rows", axis=0, tiled=True),
        lax.all_gather(value_weight, "rows", axis=0, tiled=True),
        lax.all_gather(out_weight, "rows", axis=0, tiled=True),
    )
    keys = jnp.dot(token_norm, w_key, preferred_element_type=jnp.float32).astype(jnp.bfloat16)
    values = jnp.dot(token_norm, w_value, preferred_element_type=jnp.float32).astype(jnp.bfloat16)
    head_size = D // HEADS
    heads_dev = width_dev // head_size
    latent_dev = LAT // lax.axis_size("rows")
    first_latent = lax.axis_index("rows") * latent_dev
    queries = jnp.dot(
        layer_norm(latents, latent_gain), w_query, preferred_element_type=jnp.float32
    ).astype(jnp.bfloat16)
    query_split = queries.reshape(LAT, heads_dev, head_size)
    key_split = keys.reshape(token_count, heads_dev, head_size)
    value_split = values.reshape(token_count, heads_dev, head_size)
    scores = jnp.einsum(
        "lhd,thd->lht", query_split, key_split, preferred_element_type=jnp.float32
    ) * head_size ** (-0.5)
    local_peak = jnp.max(scores, axis=2)

    def own_slice(array):
        return lax.dynamic_slice_in_dim(array, first_latent, latent_dev, 0)

    global_peak = lax.pmax(local_peak, "rows")
    weights = jnp.exp(scores - global_peak[:, :, None])
    totals = jnp.sum(weights, axis=2)
    upper_part = weights.astype(jnp.bfloat16)
    lower_part = (weights - upper_part.astype(jnp.float32)).astype(jnp.bfloat16)
    numerator = jnp.einsum(
        "lht,thd->lhd", upper_part, value_split, preferred_element_type=jnp.float32
    )
    numerator = numerator + jnp.einsum(
        "lht,thd->lhd", lower_part, value_split, preferred_element_type=jnp.float32
    )
    totals, numerator = (totals, numerator.reshape(LAT, width_dev))
    totals, numerator = lax.psum((totals, numerator), "rows")
    totals = own_slice(totals)
    numerator = own_slice(numerator)
    attended = numerator.reshape(latent_dev, heads_dev, head_size) / totals[:, :, None]
    mixed = attended.reshape(latent_dev, width_dev).astype(jnp.bfloat16)
    out_terms = lax.dot_general(
        mixed, w_out, (((1,), (1,)), ((), ())), preferred_element_type=jnp.float32
    )
    return lax.psum_scatter(out_terms, "heads", scatter_dimension=1, tiled=True).astype(
        jnp.bfloat16
    )


MESH = pl.DeviceIdType.MESH
VARIANTS = 5
F32 = jnp.float32
BF16 = jnp.bfloat16


def dot(a, b):
    return jnp.dot(a, b, preferred_element_type=F32)


def iota(shape, dim):
    return lax.broadcasted_iota(jnp.int32, shape, dim)


def over(index, power):
    return lax.shift_right_logical(index, power.bit_length() - 1)


def band_and_line(flat):
    band = jnp.zeros_like(flat)
    for step in range(1, BANDS + 1):
        band = band + (flat >= KER * step).astype(jnp.int32)
    return band, flat - KER * band


def strip_kernel(
    rows,
    heads,
    image_ref,
    stem_ref,
    token_gain_ref,
    latents_ref,
    latent_gain_ref,
    wq_ref,
    wk_ref,
    wv_ref,
    wo_ref,
    out_ref,
    image,
    stem,
    token_gain,
    latent_gain,
    latent_rows,
    latent_norm,
    query_part,
    query_in,
    lines_out,
    lines_in,
    wide,
    order,
    left,
    part_out,
    part_in,
    feature,
    w_first,
    w_second,
    kv,
    out_terms,
    out_in,
    local,
    line_s,
    line_r,
    query_s,
    query_r,
    part_s,
    part_r,
    feat_s,
    feat_r,
    end_s,
    end_r,
    z_s,
    z_r,
    gz_s,
    gz_r,
    gy_s,
    gy_r,
):
    r = lax.axis_index("rows")
    h = lax.axis_index("heads")
    core = lax.rem(h, 2)
    core_peer = h + 1 - 2 * core
    half = h // 2
    x_peer = lax.rem(h + 2, heads)
    y = lax.rem(r, 2)
    z = r // 2
    y_peer = r + 1 - 2 * y
    z_opposite = lax.rem(r + 4, rows)
    z_pair = r + 2 - 4 * lax.rem(z, 2)
    z_last = lax.rem(z_pair + 4, rows)
    own = latents_ref.shape[0] // rows
    per = stem_ref.shape[0] // KER
    pad = lines_in.shape[2]
    width = stem_ref.shape[1]
    pixels = image_ref.shape[2]
    groups = pixels // 128
    started = []

    loads = [
        pltpu.make_async_copy(source, target, local.at[k])
        for k, (source, target) in enumerate(
            [
                (image_ref, image),
                (wk_ref, w_first.at[r, 0]),
                (wv_ref, w_first.at[r, 1]),
                (stem_ref, stem),
                (wq_ref, w_second.at[r, 0]),
                (wo_ref, w_second.at[r, 1]),
                (
                    latents_ref.at[pl.ds(pl.multiple_of(z * 2 * own, 2 * own), 2 * own)],
                    latent_rows,
                ),
                (token_gain_ref, token_gain),
                (latent_gain_ref, latent_gain),
            ]
        )
    ]
    for copy in loads:
        copy.start()

    barrier = pltpu.get_barrier_semaphore()
    for d in range(1, rows):
        pl.semaphore_signal(
            barrier, inc=1, device_id=(lax.rem(r + d, rows), h), device_id_type=MESH
        )
    for d in range(1, heads):
        pl.semaphore_signal(
            barrier, inc=1, device_id=(r, lax.rem(h + d, heads)), device_id_type=MESH
        )

    quarter = pad // 2
    height = image_ref.shape[1]

    def pick(receiver, second, line):
        band, at = band_and_line(per * receiver + line)
        source = band * height + ((at + STRIDE * second) & (height - 1))
        places = iota((source.shape[0], BANDS * height), 1)
        flat = image[...].reshape(BANDS * height, pixels)
        return dot((places == source).astype(BF16), flat).astype(BF16)

    row = iota((rows * quarter, 1), 0)
    loads[0].wait()
    lines_out[...] = pick(over(row, quarter), core, half * quarter + (row & (quarter - 1))).reshape(
        lines_out.shape
    )
    pl.semaphore_wait(barrier, rows - 1 + heads - 1)

    def remote(src, dst, send, recv, to):
        copy = pltpu.make_async_remote_copy(
            src_ref=src,
            dst_ref=dst,
            send_sem=send,
            recv_sem=recv,
            device_id=to,
            device_id_type=MESH,
        )
        copy.start()
        started.append(copy)
        return copy

    def gather_start(buf, which):
        first = [
            remote(
                buf.at[r],
                buf.at[r],
                gz_s.at[which, d],
                gz_r.at[which, d],
                (lax.rem(r + 2 * d, rows), h),
            )
            for d in range(1, rows // 2)
        ]
        across = remote(
            buf.at[r], buf.at[r], gy_s.at[2 + which, 0], gy_r.at[2 + which, 0], (y_peer, h)
        )
        return first, [across]

    def gather_forward(buf, which, state):
        first, across = state
        for d, copy in enumerate(first, 1):
            copy.wait_recv()
            slot = lax.rem(r + rows - 2 * d, rows)
            across.append(
                remote(
                    buf.at[slot],
                    buf.at[slot],
                    gy_s.at[2 + which, d],
                    gy_r.at[2 + which, d],
                    (y_peer, h),
                )
            )

    def gather_wait(state):
        for copy in state[1]:
            copy.wait_recv()

    def z_start(buf, which, part):
        return [
            remote(buf.at[r], buf.at[r], z_s.at[which, 0], z_r.at[which, 0], (z_opposite, h)),
            remote(buf.at[r], buf.at[r], z_s.at[which, 1], z_r.at[which, 1], (z_pair, h)),
        ], [y_send(part(buf, r), which, 0)]

    def y_send(ref, which, k):
        return remote(ref, ref, gy_s.at[which, k], gy_r.at[which, k], (y_peer, h))

    def z_pass(buf, which, part, state):
        first, across = state
        first[0].wait_recv()
        ref = buf.at[z_opposite]
        first.append(remote(ref, ref, z_s.at[which, 2], z_r.at[which, 2], (z_pair, h)))
        across.append(y_send(part(buf, z_opposite), which, 1))
        first[1].wait_recv()
        across.append(y_send(part(buf, z_pair), which, 2))

    def z_end(buf, which, part, state):
        first, across = state
        first[2].wait_recv()
        across.append(y_send(part(buf, z_last), which, 3))

    def whole_slot(buf, slot):
        return buf.at[slot]

    def second_only(buf, slot):
        return buf.at[slot, 1]

    def lines_at(ref, slot, part):
        return ref.at[slot, core, pl.ds(pl.multiple_of(part * quarter, quarter), quarter)]

    far_first = (4, 3, 5, 2, 6, 1, 7)
    line_copies = []
    for d in far_first:
        to = lax.rem(r + d, rows)
        line_copies.append(
            remote(
                lines_out.at[to],
                lines_at(lines_in, r, half),
                line_s.at[0, d],
                line_r.at[0, d],
                (to, h),
            )
        )
    row = iota((2 * pad, 1), 0)
    lines_in[r] = pick(r, over(row, pad), row & (pad - 1)).reshape(2, pad, pixels)
    loads[1].wait()
    loads[2].wait()

    wide[...] = jnp.zeros_like(wide)
    first_state = z_start(w_first, 0, whole_slot)
    loads[3].wait()

    def widen(f, carry):
        block = stem[pl.ds(pl.multiple_of(f * KER, 16), KER), :]
        for v in range(VARIANTS - 2):
            wide[
                pl.ds(pl.multiple_of(f * 128 + STRIDE * v, 16), KER),
                v * width : (v + 1) * width,
            ] = block
        v = VARIANTS - 2
        wide[
            pl.ds(pl.multiple_of(f * 128 + STRIDE * v, 16), STRIDE),
            v * width : (v + 1) * width,
        ] = block[:STRIDE]
        v = VARIANTS - 1
        wide[
            pl.ds(pl.multiple_of(f * 128, 16), KER - STRIDE), v * width : (v + 1) * width
        ] = block[STRIDE:]
        return carry

    lax.fori_loop(0, per, widen, 0)

    token_rows = rows * TROWS
    row = iota((per * token_rows, 1), 0)
    line, token_row = over(row, token_rows), row & (token_rows - 1)
    _, at = band_and_line(per * r + line)
    odd = token_row & 1
    strip = over(token_row, 2) + jnp.where((odd == 1) & (at >= STRIDE), 1, 0)
    target = (strip * 2 + odd) * pad + line
    order[...] = (iota(order.shape, 1) == target).astype(BF16)

    def pass_line(slot, part, k, d, to):
        ref = lines_at(lines_in, slot, part)
        return remote(ref, ref, line_s.at[k, d], line_r.at[k, d], (r, to))

    over_x, over_core = [], []
    for d, copy in zip(far_first, line_copies):
        copy.wait_recv()
        slot = lax.rem(r + rows - d, rows)
        over_x.append(pass_line(slot, half, 1, d, x_peer))
        over_core.append(pass_line(slot, half, 2, d, core_peer))
    for d, copy in zip(far_first, over_x):
        copy.wait_recv()
        slot = lax.rem(r + rows - d, rows)
        over_core.append(pass_line(slot, 1 - half, 3, d, core_peer))
    loads[4].wait()
    loads[5].wait()
    second_state = z_start(w_second, 1, second_only)
    for copy in over_core:
        copy.wait_recv()
    lines = dot(order[...], lines_in[...].reshape(rows * 2 * pad, pixels)).astype(BF16)
    for f in range(per):
        for g in range(groups):
            left[g * token_rows : (g + 1) * token_rows, 128 * f : 128 * f + 128] = lines[
                f * token_rows : (f + 1) * token_rows, 128 * g : 128 * g + 128
            ]
    z_pass(w_first, 0, whole_slot, first_state)

    each = groups * TROWS
    row = iota((rows * each, 1), 0)
    strip, group, inner = over(row, each), over(row & (each - 1), TROWS), row & (TROWS - 1)
    turn = iota((rows * each, rows * each), 1) == group * token_rows + strip * TROWS + inner
    turn = turn.astype(BF16)
    part_copies = []

    def send_sums(k, sums):
        sums = jnp.concatenate(sums, axis=1).astype(BF16)
        part_out[k] = dot(turn, sums).astype(BF16).reshape(part_out.shape[1:])
        for d in far_first:
            to = lax.rem(r + d, rows)
            part_copies.append(
                remote(
                    part_out.at[k, to],
                    part_in.at[k, r],
                    part_s.at[k, d],
                    part_r.at[k, d],
                    (to, h),
                )
            )
        part_in[k, r] = part_out[k, r]

    def stem_dot(v):
        return dot(left[...], wide[:, v * width : (v + 1) * width])

    send_sums(0, [stem_dot(0), stem_dot(1)])
    rim = stem_dot(4)
    rim = jnp.concatenate([rim[token_rows:], jnp.zeros((token_rows, width), F32)], axis=0)
    send_sums(1, [stem_dot(2), stem_dot(3) + rim])

    def norm(x, gain_ref):
        average = jnp.mean(x, axis=-1, keepdims=True)
        centered = x - average
        variance = jnp.mean(centered * centered, axis=-1, keepdims=True)
        return (centered * lax.rsqrt(variance + epsilon) * gain_ref[...].astype(F32).reshape(1, -1)).astype(
            BF16
        )

    z_end(w_first, 0, whole_slot, first_state)
    for copy in loads[6:]:
        copy.wait()
    latent_norm[...] = norm(latent_rows[...].astype(F32), latent_gain)
    for copy in part_copies:
        copy.wait_recv()
    total = jnp.sum(part_in[...].astype(F32), axis=1)
    feature[h] = jnp.concatenate(
        [total[k, :, v * width : (v + 1) * width] for k in range(2) for v in range(2)], axis=0
    ).astype(BF16)

    feat_copies = []
    for d in range(1, heads):
        feat_copies.append(
            remote(
                feature.at[h],
                feature.at[h],
                feat_s.at[d],
                feat_r.at[d],
                (r, lax.rem(h + d, heads)),
            )
        )
    z_pass(w_second, 1, second_only, second_state)
    gather_wait(first_state)
    for copy in feat_copies:
        copy.wait_recv()
    token_norm = norm(
        jnp.concatenate([feature[k] for k in range(heads)], axis=1).astype(F32), token_gain
    )
    kv_states = []
    for k in range(2):
        kv[k, r] = dot(token_norm, w_first[:, k].reshape(D, width)).astype(BF16)
        kv_states.append(gather_start(kv.at[k], k))
    z_end(w_second, 1, second_only, second_state)
    depth = wq_ref.shape[0]
    part = jnp.zeros((2 * own, width), F32)
    for k in range(rows // 2):
        at = 2 * k + y
        part = part + dot(
            latent_norm[:, pl.ds(pl.multiple_of(at * depth, depth), depth)], w_second[at, 0]
        )
    query_part[...] = part.reshape(query_part.shape)
    query_copy = remote(query_part.at[1 - y], query_in, query_s, query_r, (y_peer, h))
    gather_forward(kv.at[0], 0, kv_states[0])
    query_copy.wait_recv()
    queries = (query_part[y] + query_in[...]).astype(BF16)
    gather_wait(kv_states[0])

    tokens = rows * kv.shape[2]
    keys = kv[0].reshape(tokens, width)
    size = D // HEADS
    side = iota((own, 128), 1) < size
    weights, totals = [], []
    for pair in range(width // 128):
        cols = slice(128 * pair, 128 * pair + 128)
        for keep in (side, jnp.logical_not(side)):
            mine = jnp.where(keep, queries[:, cols].astype(F32), 0.0).astype(BF16)
            scores = lax.dot_general(
                mine, keys[:, cols], (((1,), (1,)), ((), ())), preferred_element_type=F32
            ) * size ** (-0.5)
            weight = jnp.exp(scores - jnp.max(scores, axis=1, keepdims=True))
            weights.append(weight)
            totals.append(jnp.sum(weight, axis=1, keepdims=True))
    gather_forward(kv.at[1], 1, kv_states[1])
    gather_wait(kv_states[1])
    values = kv[1].reshape(tokens, width)
    mixed = []
    for pair in range(width // 128):
        v = values[:, 128 * pair : 128 * pair + 128]
        halves = []
        for k in (2 * pair, 2 * pair + 1):
            upper = weights[k].astype(BF16)
            lower = (weights[k] - upper.astype(F32)).astype(BF16)
            halves.append((dot(upper, v) + dot(lower, v)) / totals[k])
        mixed.append(jnp.where(side, halves[0], halves[1]).astype(BF16))
    mixed = jnp.concatenate(mixed, axis=1)

    gather_wait(second_state)
    for k in range(heads):
        per_head = w_second.shape[0] // heads
        block = w_second[per_head * k : per_head * (k + 1), 1].reshape(width, width)
        out_terms[k] = lax.dot_general(
            mixed, block, (((1,), (1,)), ((), ())), preferred_element_type=F32
        )
    end_copies = []
    for d in range(1, heads):
        to = lax.rem(h + d, heads)
        end_copies.append(
            remote(out_terms.at[to], out_in.at[d - 1], end_s.at[d], end_r.at[d], (r, to))
        )
    result = out_terms[h]
    for d, copy in enumerate(end_copies, 1):
        copy.wait_recv()
        result = result + out_in[d - 1]
    out_ref[...] = result.astype(BF16)
    for copy in started:
        copy.wait_send()


def fused(rows, heads):
    def per_chip(imagery, stem, token_gain, latents, latent_gain, wq, wk, wv, wo):
        per = stem.shape[0] // KER
        pad = -(-per // 16) * 16
        width = stem.shape[1]
        pixels = imagery.shape[2]
        groups = pixels // 128
        own = latents.shape[0] // rows
        tokens = TROWS * TCOLS
        token_rows = rows * TROWS
        dma = pltpu.SemaphoreType.DMA
        return pl.pallas_call(
            functools.partial(strip_kernel, rows, heads),
            out_shape=jax.ShapeDtypeStruct((own, width), BF16),
            in_specs=[pl.BlockSpec(memory_space=pltpu.HBM)] * 9,
            out_specs=pl.BlockSpec(memory_space=pltpu.VMEM),
            scratch_shapes=[
                pltpu.VMEM(imagery.shape, BF16),
                pltpu.VMEM(stem.shape, BF16),
                pltpu.VMEM((D,), BF16),
                pltpu.VMEM((D,), BF16),
                pltpu.VMEM((2 * own, D), BF16),
                pltpu.VMEM((2 * own, D), BF16),
                pltpu.VMEM((2, own, width), F32),
                pltpu.VMEM((own, width), F32),
                pltpu.VMEM((rows, pad // 2, pixels), BF16),
                pltpu.VMEM((rows, 2, pad, pixels), BF16),
                pltpu.VMEM((per * 128, VARIANTS * width), BF16),
                pltpu.VMEM((per * token_rows, rows * 2 * pad), BF16),
                pltpu.VMEM((groups * token_rows, per * 128), BF16),
                pltpu.VMEM((2, rows, groups * TROWS, 2 * width), BF16),
                pltpu.VMEM((2, rows, groups * TROWS, 2 * width), BF16),
                pltpu.VMEM((heads, tokens, width), BF16),
                pltpu.VMEM((rows, 2, wk.shape[0], width), BF16),
                pltpu.VMEM((rows, 2, wk.shape[0], width), BF16),
                pltpu.VMEM((2, rows, tokens, width), BF16),
                pltpu.VMEM((heads, own, width), F32),
                pltpu.VMEM((heads - 1, own, width), F32),
                dma((9,)),
                dma((4, rows)),
                dma((4, rows)),
                dma,
                dma,
                dma((2, rows)),
                dma((2, rows)),
                dma((heads,)),
                dma((heads,)),
                dma((heads,)),
                dma((heads,)),
                dma((2, 3)),
                dma((2, 3)),
                dma((2, rows // 2)),
                dma((2, rows // 2)),
                dma((4, rows // 2)),
                dma((4, rows // 2)),
            ],
            compiler_params=pltpu.CompilerParams(
                collective_id=0, has_side_effects=True, vmem_limit_bytes=60 * 2**20
            ),
        )(
            imagery,
            stem,
            token_gain,
            latents,
            latent_gain,
            wq,
            wk,
            wv,
            wo,
        )

    return per_chip


def lines_fit(mesh):
    return mesh.shape["rows"] == 8 and mesh.shape["heads"] == 4


def solution(mesh):
    body = fused(mesh.shape["rows"], mesh.shape["heads"]) if lines_fit(mesh) else per_device
    return jax.shard_map(
        body,
        mesh=mesh,
        in_specs=(
            P(None, "rows", None),
            P("rows", "heads"),
            P(),
            P(),
            P(),
            P("rows", "heads"),
            P("rows", "heads"),
            P("rows", "heads"),
            P("rows", "heads"),
        ),
        out_specs=P("rows", "heads"),
        check_vma=False,
    )
```

```python
import functools

import jax
import jax.numpy as jnp
from jax import lax
from jax.experimental import pallas as pl
from jax.experimental.pallas import tpu as pltpu
from jax.sharding import PartitionSpec as P

D = 1024
HEADS = 16
LAT = 512
BANDS = 5
KER = 48
STRIDE = 32
TROWS = 2
TCOLS = 32


epsilon = 1e-05


def shifted(block, axis, distance):
    devices = range(lax.axis_size(axis))
    route = [(i - distance, i) for i in devices if i - distance in devices]
    return lax.ppermute(block, axis, route)


def layer_norm(inputs, gain_row):
    widened = inputs.astype(jnp.float32)
    average = jnp.mean(widened, axis=-1, keepdims=True)
    centered = widened - average
    variance = jnp.mean(centered * centered, axis=-1, keepdims=True)
    return (centered * lax.rsqrt(variance + epsilon) * gain_row.astype(jnp.float32)).astype(
        jnp.bfloat16
    )


def build_patches(strip_rows):
    rim_rows = KER - STRIDE
    padded = jnp.pad(strip_rows, ((0, 0), (0, STRIDE - rim_rows), (0, STRIDE)))
    blocks = padded.reshape(BANDS, TROWS + 1, STRIDE, TCOLS + 1, STRIDE)
    row_cat = jnp.concatenate([blocks[:, :TROWS], blocks[:, 1:, :rim_rows]], axis=2)
    col_cat = jnp.concatenate(
        [row_cat[:, :, :, :TCOLS, :], row_cat[:, :, :, 1:, :rim_rows]], axis=4
    )
    ordered = jnp.transpose(col_cat, (1, 3, 0, 2, 4))
    return ordered.reshape(TROWS * TCOLS, BANDS * KER * KER)


def per_device(
    imagery,
    stem_weight,
    token_gain,
    latents,
    latent_gain,
    query_weight,
    key_weight,
    value_weight,
    out_weight,
):
    rim_rows = KER - STRIDE
    below = shifted(imagery[:, :rim_rows, :], "rows", -1)
    patches = build_patches(jnp.concatenate([imagery, below], axis=1))
    token_count = patches.shape[0]
    width_dev = stem_weight.shape[1]
    stem_out = jnp.dot(
        patches,
        lax.all_gather(stem_weight, "rows", axis=0, tiled=True),
        preferred_element_type=jnp.float32,
    )
    feature = lax.all_gather(stem_out.astype(jnp.bfloat16), "heads", axis=1, tiled=True)
    token_norm = layer_norm(feature, token_gain)
    w_query, w_key, w_value, w_out = (
        lax.all_gather(query_weight, "rows", axis=0, tiled=True),
        lax.all_gather(key_weight, "rows", axis=0, tiled=True),
        lax.all_gather(value_weight, "rows", axis=0, tiled=True),
        lax.all_gather(out_weight, "rows", axis=0, tiled=True),
    )
    keys = jnp.dot(token_norm, w_key, preferred_element_type=jnp.float32).astype(jnp.bfloat16)
    values = jnp.dot(token_norm, w_value, preferred_element_type=jnp.float32).astype(jnp.bfloat16)
    head_size = D // HEADS
    heads_dev = width_dev // head_size
    latent_dev = LAT // lax.axis_size("rows")
    first_latent = lax.axis_index("rows") * latent_dev
    queries = jnp.dot(
        layer_norm(latents, latent_gain), w_query, preferred_element_type=jnp.float32
    ).astype(jnp.bfloat16)
    query_split = queries.reshape(LAT, heads_dev, head_size)
    key_split = keys.reshape(token_count, heads_dev, head_size)
    value_split = values.reshape(token_count, heads_dev, head_size)
    scores = jnp.einsum(
        "lhd,thd->lht", query_split, key_split, preferred_element_type=jnp.float32
    ) * head_size ** (-0.5)
    local_peak = jnp.max(scores, axis=2)

    def own_slice(array):
        return lax.dynamic_slice_in_dim(array, first_latent, latent_dev, 0)

    global_peak = lax.pmax(local_peak, "rows")
    weights = jnp.exp(scores - global_peak[:, :, None])
    totals = jnp.sum(weights, axis=2)
    upper_part = weights.astype(jnp.bfloat16)
    lower_part = (weights - upper_part.astype(jnp.float32)).astype(jnp.bfloat16)
    numerator = jnp.einsum(
        "lht,thd->lhd", upper_part, value_split, preferred_element_type=jnp.float32
    )
    numerator = numerator + jnp.einsum(
        "lht,thd->lhd", lower_part, value_split, preferred_element_type=jnp.float32
    )
    totals, numerator = (totals, numerator.reshape(LAT, width_dev))
    totals, numerator = lax.psum((totals, numerator), "rows")
    totals = own_slice(totals)
    numerator = own_slice(numerator)
    attended = numerator.reshape(latent_dev, heads_dev, head_size) / totals[:, :, None]
    mixed = attended.reshape(latent_dev, width_dev).astype(jnp.bfloat16)
    out_terms = lax.dot_general(
        mixed, w_out, (((1,), (1,)), ((), ())), preferred_element_type=jnp.float32
    )
    return lax.psum_scatter(out_terms, "heads", scatter_dimension=1, tiled=True).astype(
        jnp.bfloat16
    )


MESH = pl.DeviceIdType.MESH
VARIANTS = 5
F32 = jnp.float32
BF16 = jnp.bfloat16


def dot(a, b):
    return jnp.dot(a, b, preferred_element_type=F32)


def iota(shape, dim):
    return lax.broadcasted_iota(jnp.int32, shape, dim)


def over(index, power):
    return lax.shift_right_logical(index, power.bit_length() - 1)


def band_and_line(flat):
    band = jnp.zeros_like(flat)
    for step in range(1, BANDS + 1):
        band = band + (flat >= KER * step).astype(jnp.int32)
    return band, flat - KER * band


def strip_kernel(
    rows,
    heads,
    image_ref,
    stem_ref,
    token_gain_ref,
    latents_ref,
    latent_gain_ref,
    wq_ref,
    wk_ref,
    wv_ref,
    wo_ref,
    out_ref,
    image,
    stem,
    token_gain,
    latent_gain,
    latent_rows,
    latent_norm,
    query_part,
    query_in,
    lines_out,
    lines_in,
    wide,
    order,
    left,
    part_out,
    part_in,
    feature,
    w_first,
    w_query,
    w_out,
    kv,
    out_terms,
    out_in,
    local,
    line_s,
    line_r,
    query_s,
    query_r,
    part_s,
    part_r,
    feat_s,
    feat_r,
    end_s,
    end_r,
    z_s,
    z_r,
    gz_s,
    gz_r,
    gy_s,
    gy_r,
):
    r = lax.axis_index("rows")
    h = lax.axis_index("heads")
    core = lax.rem(h, 2)
    core_peer = h + 1 - 2 * core
    half = h // 2
    x_peer = lax.rem(h + 2, heads)
    y = lax.rem(r, 2)
    z = r // 2
    y_peer = r + 1 - 2 * y
    z_opposite = lax.rem(r + 4, rows)
    z_pair = r + 2 - 4 * lax.rem(z, 2)
    z_last = lax.rem(z_pair + 4, rows)
    own = latents_ref.shape[0] // rows
    per = stem_ref.shape[0] // KER
    pad = lines_in.shape[2]
    width = stem_ref.shape[1]
    pixels = image_ref.shape[2]
    groups = pixels // 128
    started = []

    loads = [
        pltpu.make_async_copy(source, target, local.at[k])
        for k, (source, target) in enumerate(
            [
                (image_ref, image),
                (wk_ref, w_first.at[r, 0]),
                (wv_ref, w_first.at[r, 1]),
                (stem_ref, stem),
                (wq_ref, w_query.at[r]),
                (wo_ref, w_out.at[r]),
                (
                    latents_ref.at[pl.ds(pl.multiple_of(z * 2 * own, 2 * own), 2 * own)],
                    latent_rows,
                ),
                (token_gain_ref, token_gain),
                (latent_gain_ref, latent_gain),
            ]
        )
    ]
    for copy in loads:
        copy.start()

    barrier = pltpu.get_barrier_semaphore()
    for d in range(1, rows):
        pl.semaphore_signal(
            barrier, inc=1, device_id=(lax.rem(r + d, rows), h), device_id_type=MESH
        )
    for d in range(1, heads):
        pl.semaphore_signal(
            barrier, inc=1, device_id=(r, lax.rem(h + d, heads)), device_id_type=MESH
        )

    quarter = pad // 2
    height = image_ref.shape[1]

    def pick(receiver, second, line):
        band, at = band_and_line(per * receiver + line)
        source = band * height + ((at + STRIDE * second) & (height - 1))
        places = iota((source.shape[0], BANDS * height), 1)
        flat = image[...].reshape(BANDS * height, pixels)
        return dot((places == source).astype(BF16), flat).astype(BF16)

    row = iota((rows * quarter, 1), 0)
    wide[...] = jnp.zeros_like(wide)
    loads[0].wait()
    lines_out[...] = pick(over(row, quarter), core, half * quarter + (row & (quarter - 1))).reshape(
        lines_out.shape
    )
    pl.semaphore_wait(barrier, rows - 1 + heads - 1)

    def remote(src, dst, send, recv, to):
        copy = pltpu.make_async_remote_copy(
            src_ref=src,
            dst_ref=dst,
            send_sem=send,
            recv_sem=recv,
            device_id=to,
            device_id_type=MESH,
        )
        copy.start()
        started.append(copy)
        return copy

    def gather_start(buf, which):
        first = [
            remote(
                buf.at[r],
                buf.at[r],
                gz_s.at[which, d],
                gz_r.at[which, d],
                (lax.rem(r + 2 * d, rows), h),
            )
            for d in range(1, rows // 2)
        ]
        across = remote(
            buf.at[r], buf.at[r], gy_s.at[3 + which, 0], gy_r.at[3 + which, 0], (y_peer, h)
        )
        return first, [across]

    def gather_forward(buf, which, state):
        first, across = state
        for d, copy in enumerate(first, 1):
            copy.wait_recv()
            slot = lax.rem(r + rows - 2 * d, rows)
            across.append(
                remote(
                    buf.at[slot],
                    buf.at[slot],
                    gy_s.at[3 + which, d],
                    gy_r.at[3 + which, d],
                    (y_peer, h),
                )
            )

    def gather_wait(state):
        for copy in state[1]:
            copy.wait_recv()

    def z_start(buf, which, over_y=True):
        first = [
            remote(buf.at[r], buf.at[r], z_s.at[which, 0], z_r.at[which, 0], (z_opposite, h)),
            remote(buf.at[r], buf.at[r], z_s.at[which, 1], z_r.at[which, 1], (z_pair, h)),
        ]
        across = []

        def y_send(slot):
            k = len(across)
            if over_y:
                ref = buf.at[slot]
                across.append(
                    remote(ref, ref, gy_s.at[which, k], gy_r.at[which, k], (y_peer, h))
                )

        y_send(r)
        return buf, which, first, across, y_send

    def z_pass(state):
        buf, which, first, across, y_send = state
        first[0].wait_recv()
        ref = buf.at[z_opposite]
        first.append(remote(ref, ref, z_s.at[which, 2], z_r.at[which, 2], (z_pair, h)))
        y_send(z_opposite)
        first[1].wait_recv()
        y_send(z_pair)

    def z_end(state):
        buf, which, first, across, y_send = state
        first[2].wait_recv()
        y_send(z_last)

    def lines_at(ref, slot, part):
        return ref.at[slot, core, pl.ds(pl.multiple_of(part * quarter, quarter), quarter)]

    far_first = (4, 3, 5, 2, 6, 1, 7)
    line_copies = []
    for d in far_first:
        to = lax.rem(r + d, rows)
        line_copies.append(
            remote(
                lines_out.at[to],
                lines_at(lines_in, r, half),
                line_s.at[0, d],
                line_r.at[0, d],
                (to, h),
            )
        )
    row = iota((2 * pad, 1), 0)
    lines_in[r] = pick(r, over(row, pad), row & (pad - 1)).reshape(2, pad, pixels)
    def widen(f, carry):
        block = stem[pl.ds(pl.multiple_of(f * KER, 16), KER), :]
        for v in range(VARIANTS - 2):
            wide[
                pl.ds(pl.multiple_of(f * 128 + STRIDE * v, 16), KER),
                v * width : (v + 1) * width,
            ] = block
        v = VARIANTS - 2
        wide[
            pl.ds(pl.multiple_of(f * 128 + STRIDE * v, 16), STRIDE),
            v * width : (v + 1) * width,
        ] = block[:STRIDE]
        v = VARIANTS - 1
        wide[
            pl.ds(pl.multiple_of(f * 128, 16), KER - STRIDE), v * width : (v + 1) * width
        ] = block[STRIDE:]
        return carry

    token_rows = rows * TROWS
    row = iota((per * token_rows, 1), 0)
    line, token_row = over(row, token_rows), row & (token_rows - 1)
    _, at = band_and_line(per * r + line)
    odd = token_row & 1
    strip = over(token_row, 2) + jnp.where((odd == 1) & (at >= STRIDE), 1, 0)
    target = (strip * 2 + odd) * pad + line
    order[...] = (iota(order.shape, 1) == target).astype(BF16)

    def pass_line(slot, part, k, d, to):
        ref = lines_at(lines_in, slot, part)
        return remote(ref, ref, line_s.at[k, d], line_r.at[k, d], (r, to))

    over_x, over_core = [], []
    loads[3].wait()
    parts = len(far_first)
    for k, (d, copy) in enumerate(zip(far_first, line_copies)):
        lax.fori_loop(per * k // parts, per * (k + 1) // parts, widen, 0)
        copy.wait_recv()
        slot = lax.rem(r + rows - d, rows)
        over_x.append(pass_line(slot, half, 1, d, x_peer))
        over_core.append(pass_line(slot, half, 2, d, core_peer))
    loads[1].wait()
    loads[2].wait()
    first_state = z_start(w_first, 0)
    for d, copy in zip(far_first, over_x):
        copy.wait_recv()
        slot = lax.rem(r + rows - d, rows)
        over_core.append(pass_line(slot, 1 - half, 3, d, core_peer))
    for copy in over_core:
        copy.wait_recv()
    lines = dot(order[...], lines_in[...].reshape(rows * 2 * pad, pixels)).astype(BF16)
    for f in range(per):
        for g in range(groups):
            left[g * token_rows : (g + 1) * token_rows, 128 * f : 128 * f + 128] = lines[
                f * token_rows : (f + 1) * token_rows, 128 * g : 128 * g + 128
            ]
    z_pass(first_state)

    each = groups * TROWS
    row = iota((rows * each, 1), 0)
    strip, group, inner = over(row, each), over(row & (each - 1), TROWS), row & (TROWS - 1)
    turn = iota((rows * each, rows * each), 1) == group * token_rows + strip * TROWS + inner
    turn = turn.astype(BF16)
    part_copies = []

    def send_sums(k, sums):
        sums = jnp.concatenate(sums, axis=1).astype(BF16)
        part_out[k] = dot(turn, sums).astype(BF16).reshape(part_out.shape[1:])
        for d in far_first:
            to = lax.rem(r + d, rows)
            part_copies.append(
                remote(
                    part_out.at[k, to],
                    part_in.at[k, r],
                    part_s.at[k, d],
                    part_r.at[k, d],
                    (to, h),
                )
            )
        part_in[k, r] = part_out[k, r]

    def stem_dot(v):
        return dot(left[...], wide[:, v * width : (v + 1) * width])

    send_sums(0, [stem_dot(0), stem_dot(1)])
    rim = stem_dot(4)
    rim = jnp.concatenate([rim[token_rows:], jnp.zeros((token_rows, width), F32)], axis=0)
    send_sums(1, [stem_dot(2), stem_dot(3) + rim])
    loads[4].wait()
    query_state = z_start(w_query, 1, over_y=False)

    def norm(x, gain_ref):
        average = jnp.mean(x, axis=-1, keepdims=True)
        centered = x - average
        variance = jnp.mean(centered * centered, axis=-1, keepdims=True)
        return (centered * lax.rsqrt(variance + epsilon) * gain_ref[...].astype(F32).reshape(1, -1)).astype(
            BF16
        )

    z_end(first_state)
    for copy in loads[6:]:
        copy.wait()
    latent_norm[...] = norm(latent_rows[...].astype(F32), latent_gain)
    for copy in part_copies:
        copy.wait_recv()
    total = jnp.sum(part_in[...].astype(F32), axis=1)
    feature[h] = jnp.concatenate(
        [total[k, :, v * width : (v + 1) * width] for k in range(2) for v in range(2)], axis=0
    ).astype(BF16)

    feat_copies = []
    for d in range(1, heads):
        feat_copies.append(
            remote(
                feature.at[h],
                feature.at[h],
                feat_s.at[d],
                feat_r.at[d],
                (r, lax.rem(h + d, heads)),
            )
        )
    loads[5].wait()
    out_state = z_start(w_out, 2)
    z_pass(query_state)
    gather_wait(first_state[2:])
    for copy in feat_copies:
        copy.wait_recv()
    token_norm = norm(
        jnp.concatenate([feature[k] for k in range(heads)], axis=1).astype(F32), token_gain
    )
    kv_states = []
    for k in range(2):
        kv[k, r] = dot(token_norm, w_first[:, k].reshape(D, width)).astype(BF16)
        kv_states.append(gather_start(kv.at[k], k))
    z_end(query_state)
    depth = wq_ref.shape[0]
    part = jnp.zeros((2 * own, width), F32)
    for k in range(rows // 2):
        at = 2 * k + y
        part = part + dot(
            latent_norm[:, pl.ds(pl.multiple_of(at * depth, depth), depth)], w_query[at]
        )
    query_part[...] = part.reshape(query_part.shape)
    query_copy = remote(query_part.at[1 - y], query_in, query_s, query_r, (y_peer, h))
    z_pass(out_state)
    gather_forward(kv.at[0], 0, kv_states[0])
    query_copy.wait_recv()
    queries = (query_part[y] + query_in[...]).astype(BF16)
    gather_wait(kv_states[0])

    tokens = rows * kv.shape[2]
    keys = kv[0].reshape(tokens, width)
    size = D // HEADS
    side = iota((own, 128), 1) < size
    weights, totals = [], []
    for pair in range(width // 128):
        cols = slice(128 * pair, 128 * pair + 128)
        for keep in (side, jnp.logical_not(side)):
            mine = jnp.where(keep, queries[:, cols].astype(F32), 0.0).astype(BF16)
            scores = lax.dot_general(
                mine, keys[:, cols], (((1,), (1,)), ((), ())), preferred_element_type=F32
            ) * size ** (-0.5)
            weight = jnp.exp(scores - jnp.max(scores, axis=1, keepdims=True))
            weights.append(weight)
            totals.append(jnp.sum(weight, axis=1, keepdims=True))
    gather_forward(kv.at[1], 1, kv_states[1])
    z_end(out_state)
    gather_wait(kv_states[1])
    values = kv[1].reshape(tokens, width)
    mixed = []
    for pair in range(width // 128):
        v = values[:, 128 * pair : 128 * pair + 128]
        halves = []
        for k in (2 * pair, 2 * pair + 1):
            upper = weights[k].astype(BF16)
            lower = (weights[k] - upper.astype(F32)).astype(BF16)
            halves.append((dot(upper, v) + dot(lower, v)) / totals[k])
        mixed.append(jnp.where(side, halves[0], halves[1]).astype(BF16))
    mixed = jnp.concatenate(mixed, axis=1)

    gather_wait(out_state[2:])
    for k in range(heads):
        per_head = w_out.shape[0] // heads
        block = w_out[per_head * k : per_head * (k + 1)].reshape(width, width)
        out_terms[k] = lax.dot_general(
            mixed, block, (((1,), (1,)), ((), ())), preferred_element_type=F32
        )
    end_copies = []
    for d in range(1, heads):
        to = lax.rem(h + d, heads)
        end_copies.append(
            remote(out_terms.at[to], out_in.at[d - 1], end_s.at[d], end_r.at[d], (r, to))
        )
    result = out_terms[h]
    for d, copy in enumerate(end_copies, 1):
        copy.wait_recv()
        result = result + out_in[d - 1]
    out_ref[...] = result.astype(BF16)
    for copy in started:
        copy.wait_send()


def fused(rows, heads):
    def per_chip(imagery, stem, token_gain, latents, latent_gain, wq, wk, wv, wo):
        per = stem.shape[0] // KER
        pad = -(-per // 16) * 16
        width = stem.shape[1]
        pixels = imagery.shape[2]
        groups = pixels // 128
        own = latents.shape[0] // rows
        tokens = TROWS * TCOLS
        token_rows = rows * TROWS
        dma = pltpu.SemaphoreType.DMA
        return pl.pallas_call(
            functools.partial(strip_kernel, rows, heads),
            out_shape=jax.ShapeDtypeStruct((own, width), BF16),
            in_specs=[pl.BlockSpec(memory_space=pltpu.HBM)] * 9,
            out_specs=pl.BlockSpec(memory_space=pltpu.VMEM),
            scratch_shapes=[
                pltpu.VMEM(imagery.shape, BF16),
                pltpu.VMEM(stem.shape, BF16),
                pltpu.VMEM((D,), BF16),
                pltpu.VMEM((D,), BF16),
                pltpu.VMEM((2 * own, D), BF16),
                pltpu.VMEM((2 * own, D), BF16),
                pltpu.VMEM((2, own, width), F32),
                pltpu.VMEM((own, width), F32),
                pltpu.VMEM((rows, pad // 2, pixels), BF16),
                pltpu.VMEM((rows, 2, pad, pixels), BF16),
                pltpu.VMEM((per * 128, VARIANTS * width), BF16),
                pltpu.VMEM((per * token_rows, rows * 2 * pad), BF16),
                pltpu.VMEM((groups * token_rows, per * 128), BF16),
                pltpu.VMEM((2, rows, groups * TROWS, 2 * width), BF16),
                pltpu.VMEM((2, rows, groups * TROWS, 2 * width), BF16),
                pltpu.VMEM((heads, tokens, width), BF16),
                pltpu.VMEM((rows, 2, wk.shape[0], width), BF16),
                pltpu.VMEM((rows, wq.shape[0], width), BF16),
                pltpu.VMEM((rows, wo.shape[0], width), BF16),
                pltpu.VMEM((2, rows, tokens, width), BF16),
                pltpu.VMEM((heads, own, width), F32),
                pltpu.VMEM((heads - 1, own, width), F32),
                dma((9,)),
                dma((4, rows)),
                dma((4, rows)),
                dma,
                dma,
                dma((2, rows)),
                dma((2, rows)),
                dma((heads,)),
                dma((heads,)),
                dma((heads,)),
                dma((heads,)),
                dma((3, 3)),
                dma((3, 3)),
                dma((2, rows // 2)),
                dma((2, rows // 2)),
                dma((5, rows // 2)),
                dma((5, rows // 2)),
            ],
            compiler_params=pltpu.CompilerParams(
                collective_id=0, has_side_effects=True, vmem_limit_bytes=60 * 2**20
            ),
        )(
            imagery,
            stem,
            token_gain,
            latents,
            latent_gain,
            wq,
            wk,
            wv,
            wo,
        )

    return per_chip


def lines_fit(mesh):
    return mesh.shape["rows"] == 8 and mesh.shape["heads"] == 4


def solution(mesh):
    body = fused(mesh.shape["rows"], mesh.shape["heads"]) if lines_fit(mesh) else per_device
    return jax.shard_map(
        body,
        mesh=mesh,
        in_specs=(
            P(None, "rows", None),
            P("rows", "heads"),
            P(),
            P(),
            P(),
            P("rows", "heads"),
            P("rows", "heads"),
            P("rows", "heads"),
            P("rows", "heads"),
        ),
        out_specs=P("rows", "heads"),
        check_vma=False,
    )
```

```python
import functools

import jax
import jax.numpy as jnp
from jax import lax
from jax.experimental import pallas as pl
from jax.experimental.pallas import tpu as pltpu
from jax.sharding import PartitionSpec as P

D = 1024
HEADS = 16
LAT = 512
BANDS = 5
KER = 48
STRIDE = 32
TROWS = 2
TCOLS = 32


epsilon = 1e-05


def shifted(block, axis, distance):
    devices = range(lax.axis_size(axis))
    route = [(i - distance, i) for i in devices if i - distance in devices]
    return lax.ppermute(block, axis, route)


def layer_norm(inputs, gain_row):
    widened = inputs.astype(jnp.float32)
    average = jnp.mean(widened, axis=-1, keepdims=True)
    centered = widened - average
    variance = jnp.mean(centered * centered, axis=-1, keepdims=True)
    return (centered * lax.rsqrt(variance + epsilon) * gain_row.astype(jnp.float32)).astype(
        jnp.bfloat16
    )


def build_patches(strip_rows):
    rim_rows = KER - STRIDE
    padded = jnp.pad(strip_rows, ((0, 0), (0, STRIDE - rim_rows), (0, STRIDE)))
    blocks = padded.reshape(BANDS, TROWS + 1, STRIDE, TCOLS + 1, STRIDE)
    row_cat = jnp.concatenate([blocks[:, :TROWS], blocks[:, 1:, :rim_rows]], axis=2)
    col_cat = jnp.concatenate(
        [row_cat[:, :, :, :TCOLS, :], row_cat[:, :, :, 1:, :rim_rows]], axis=4
    )
    ordered = jnp.transpose(col_cat, (1, 3, 0, 2, 4))
    return ordered.reshape(TROWS * TCOLS, BANDS * KER * KER)


def per_device(
    imagery,
    stem_weight,
    token_gain,
    latents,
    latent_gain,
    query_weight,
    key_weight,
    value_weight,
    out_weight,
):
    rim_rows = KER - STRIDE
    below = shifted(imagery[:, :rim_rows, :], "rows", -1)
    patches = build_patches(jnp.concatenate([imagery, below], axis=1))
    token_count = patches.shape[0]
    width_dev = stem_weight.shape[1]
    stem_out = jnp.dot(
        patches,
        lax.all_gather(stem_weight, "rows", axis=0, tiled=True),
        preferred_element_type=jnp.float32,
    )
    feature = lax.all_gather(stem_out.astype(jnp.bfloat16), "heads", axis=1, tiled=True)
    token_norm = layer_norm(feature, token_gain)
    w_query, w_key, w_value, w_out = (
        lax.all_gather(query_weight, "rows", axis=0, tiled=True),
        lax.all_gather(key_weight, "rows", axis=0, tiled=True),
        lax.all_gather(value_weight, "rows", axis=0, tiled=True),
        lax.all_gather(out_weight, "rows", axis=0, tiled=True),
    )
    keys = jnp.dot(token_norm, w_key, preferred_element_type=jnp.float32).astype(jnp.bfloat16)
    values = jnp.dot(token_norm, w_value, preferred_element_type=jnp.float32).astype(jnp.bfloat16)
    head_size = D // HEADS
    heads_dev = width_dev // head_size
    latent_dev = LAT // lax.axis_size("rows")
    first_latent = lax.axis_index("rows") * latent_dev
    queries = jnp.dot(
        layer_norm(latents, latent_gain), w_query, preferred_element_type=jnp.float32
    ).astype(jnp.bfloat16)
    query_split = queries.reshape(LAT, heads_dev, head_size)
    key_split = keys.reshape(token_count, heads_dev, head_size)
    value_split = values.reshape(token_count, heads_dev, head_size)
    scores = jnp.einsum(
        "lhd,thd->lht", query_split, key_split, preferred_element_type=jnp.float32
    ) * head_size ** (-0.5)
    local_peak = jnp.max(scores, axis=2)

    def own_slice(array):
        return lax.dynamic_slice_in_dim(array, first_latent, latent_dev, 0)

    global_peak = lax.pmax(local_peak, "rows")
    weights = jnp.exp(scores - global_peak[:, :, None])
    totals = jnp.sum(weights, axis=2)
    upper_part = weights.astype(jnp.bfloat16)
    lower_part = (weights - upper_part.astype(jnp.float32)).astype(jnp.bfloat16)
    numerator = jnp.einsum(
        "lht,thd->lhd", upper_part, value_split, preferred_element_type=jnp.float32
    )
    numerator = numerator + jnp.einsum(
        "lht,thd->lhd", lower_part, value_split, preferred_element_type=jnp.float32
    )
    totals, numerator = (totals, numerator.reshape(LAT, width_dev))
    totals, numerator = lax.psum((totals, numerator), "rows")
    totals = own_slice(totals)
    numerator = own_slice(numerator)
    attended = numerator.reshape(latent_dev, heads_dev, head_size) / totals[:, :, None]
    mixed = attended.reshape(latent_dev, width_dev).astype(jnp.bfloat16)
    out_terms = lax.dot_general(
        mixed, w_out, (((1,), (1,)), ((), ())), preferred_element_type=jnp.float32
    )
    return lax.psum_scatter(out_terms, "heads", scatter_dimension=1, tiled=True).astype(
        jnp.bfloat16
    )


MESH = pl.DeviceIdType.MESH
VARIANTS = 5
F32 = jnp.float32
BF16 = jnp.bfloat16


def dot(a, b):
    return jnp.dot(a, b, preferred_element_type=F32)


def iota(shape, dim):
    return lax.broadcasted_iota(jnp.int32, shape, dim)


def over(index, power):
    return lax.shift_right_logical(index, power.bit_length() - 1)


def band_and_line(flat):
    band = jnp.zeros_like(flat)
    for step in range(1, BANDS + 1):
        band = band + (flat >= KER * step).astype(jnp.int32)
    return band, flat - KER * band


def strip_kernel(
    rows,
    heads,
    image_ref,
    stem_ref,
    token_gain_ref,
    latents_ref,
    latent_gain_ref,
    wq_ref,
    wk_ref,
    wv_ref,
    wo_ref,
    out_ref,
    image,
    stem,
    token_gain,
    latent_gain,
    latent_rows,
    latent_norm,
    query_part,
    query_in,
    lines_out,
    lines_in,
    wide,
    order,
    left,
    stem_sum,
    part_out,
    part_in,
    feature,
    w_first,
    w_query,
    w_out,
    kv,
    out_terms,
    out_in,
    local,
    line_s,
    line_r,
    query_s,
    query_r,
    part_s,
    part_r,
    feat_s,
    feat_r,
    end_s,
    end_r,
    z_s,
    z_r,
    gz_s,
    gz_r,
    gy_s,
    gy_r,
):
    r = lax.axis_index("rows")
    h = lax.axis_index("heads")
    core = lax.rem(h, 2)
    core_peer = h + 1 - 2 * core
    half = h // 2
    x_peer = lax.rem(h + 2, heads)
    y = lax.rem(r, 2)
    z = r // 2
    y_peer = r + 1 - 2 * y
    z_opposite = lax.rem(r + 4, rows)
    z_pair = r + 2 - 4 * lax.rem(z, 2)
    z_last = lax.rem(z_pair + 4, rows)
    own = latents_ref.shape[0] // rows
    per = stem_ref.shape[0] // KER
    quarter = lines_in.shape[3]
    width = stem_ref.shape[1]
    pixels = image_ref.shape[2]
    groups = pixels // 128
    started = []

    loads = [
        pltpu.make_async_copy(source, target, local.at[k])
        for k, (source, target) in enumerate(
            [
                (image_ref, image),
                (wk_ref, w_first.at[r, 0]),
                (wv_ref, w_first.at[r, 1]),
                (stem_ref, stem),
                (wq_ref, w_query.at[r]),
                (wo_ref, w_out.at[r]),
                (
                    latents_ref.at[pl.ds(pl.multiple_of(z * 2 * own, 2 * own), 2 * own)],
                    latent_rows,
                ),
                (token_gain_ref, token_gain),
                (latent_gain_ref, latent_gain),
            ]
        )
    ]
    for copy in loads:
        copy.start()

    barrier = pltpu.get_barrier_semaphore()
    for d in range(1, rows):
        pl.semaphore_signal(
            barrier, inc=1, device_id=(lax.rem(r + d, rows), h), device_id_type=MESH
        )
    for d in range(1, heads):
        pl.semaphore_signal(
            barrier, inc=1, device_id=(r, lax.rem(h + d, heads)), device_id_type=MESH
        )

    height = image_ref.shape[1]

    def pick(receiver, second, line):
        band, at = band_and_line(per * receiver + line)
        source = band * height + ((at + STRIDE * second) & (height - 1))
        places = iota((source.shape[0], BANDS * height), 1)
        flat = image[...].reshape(BANDS * height, pixels)
        return dot((places == source).astype(BF16), flat).astype(BF16)

    row = iota((rows * quarter, 1), 0)
    wide[...] = jnp.zeros_like(wide)
    loads[0].wait()
    lines_out[...] = pick(over(row, quarter), core, half * quarter + (row & (quarter - 1))).reshape(
        lines_out.shape
    )
    pl.semaphore_wait(barrier, rows - 1 + heads - 1)

    def remote(src, dst, send, recv, to):
        copy = pltpu.make_async_remote_copy(
            src_ref=src,
            dst_ref=dst,
            send_sem=send,
            recv_sem=recv,
            device_id=to,
            device_id_type=MESH,
        )
        copy.start()
        started.append(copy)
        return copy

    def gather_start(buf, which):
        first = [
            remote(
                buf.at[r],
                buf.at[r],
                gz_s.at[which, d],
                gz_r.at[which, d],
                (lax.rem(r + 2 * d, rows), h),
            )
            for d in range(1, rows // 2)
        ]
        across = remote(
            buf.at[r], buf.at[r], gy_s.at[3 + which, 0], gy_r.at[3 + which, 0], (y_peer, h)
        )
        return first, [across]

    def gather_forward(buf, which, state):
        first, across = state
        for d, copy in enumerate(first, 1):
            copy.wait_recv()
            slot = lax.rem(r + rows - 2 * d, rows)
            across.append(
                remote(
                    buf.at[slot],
                    buf.at[slot],
                    gy_s.at[3 + which, d],
                    gy_r.at[3 + which, d],
                    (y_peer, h),
                )
            )

    def gather_wait(state):
        for copy in state[1]:
            copy.wait_recv()

    def z_start(buf, which, over_y=True):
        first = [
            remote(buf.at[r], buf.at[r], z_s.at[which, 0], z_r.at[which, 0], (z_opposite, h)),
            remote(buf.at[r], buf.at[r], z_s.at[which, 1], z_r.at[which, 1], (z_pair, h)),
        ]
        across = []

        def y_send(slot):
            k = len(across)
            if over_y:
                ref = buf.at[slot]
                across.append(
                    remote(ref, ref, gy_s.at[which, k], gy_r.at[which, k], (y_peer, h))
                )

        y_send(r)
        return buf, which, first, across, y_send

    def z_pass(state):
        buf, which, first, across, y_send = state
        first[0].wait_recv()
        ref = buf.at[z_opposite]
        first.append(remote(ref, ref, z_s.at[which, 2], z_r.at[which, 2], (z_pair, h)))
        y_send(z_opposite)
        first[1].wait_recv()
        y_send(z_pair)

    def z_end(state):
        buf, which, first, across, y_send = state
        first[2].wait_recv()
        y_send(z_last)

    far_first = (4, 3, 5, 2, 6, 1, 7)
    line_copies = []
    for d in far_first:
        to = lax.rem(r + d, rows)
        line_copies.append(
            remote(
                lines_out.at[to],
                lines_in.at[half, r, core],
                line_s.at[0, d],
                line_r.at[0, d],
                (to, h),
            )
        )
    for part in range(2):
        row = iota((2 * quarter, 1), 0)
        lines_in[part, r] = pick(
            r, over(row, quarter), part * quarter + (row & (quarter - 1))
        ).reshape(2, quarter, pixels)
    def widen(f, carry):
        block = stem[pl.ds(pl.multiple_of(f * KER, 16), KER), :]
        for v in range(VARIANTS - 2):
            wide[
                pl.ds(pl.multiple_of(f * 128 + STRIDE * v, 16), KER),
                v * width : (v + 1) * width,
            ] = block
        v = VARIANTS - 2
        wide[
            pl.ds(pl.multiple_of(f * 128 + STRIDE * v, 16), STRIDE),
            v * width : (v + 1) * width,
        ] = block[:STRIDE]
        v = VARIANTS - 1
        wide[
            pl.ds(pl.multiple_of(f * 128, 16), KER - STRIDE), v * width : (v + 1) * width
        ] = block[STRIDE:]
        return carry

    token_rows = rows * TROWS
    row = iota((quarter * token_rows, 1), 0)
    line, token_row = over(row, token_rows), row & (token_rows - 1)
    odd = token_row & 1
    for part in range(2):
        _, at = band_and_line(per * r + part * quarter + line)
        strip = over(token_row, 2) + jnp.where((odd == 1) & (at >= STRIDE), 1, 0)
        target = (strip * 2 + odd) * quarter + line
        order[part] = (iota(order.shape[1:], 1) == target).astype(BF16)

    def pass_line(slot, part, k, d, to):
        ref = lines_in.at[part, slot, core]
        return remote(ref, ref, line_s.at[k, d], line_r.at[k, d], (r, to))

    over_x, over_core = [], []
    loads[3].wait()
    parts = len(far_first)
    for k, (d, copy) in enumerate(zip(far_first, line_copies)):
        lax.fori_loop(per * k // parts, per * (k + 1) // parts, widen, 0)
        copy.wait_recv()
        slot = lax.rem(r + rows - d, rows)
        over_x.append(pass_line(slot, half, 1, d, x_peer))
        over_core.append(pass_line(slot, half, 2, d, core_peer))
    loads[1].wait()
    loads[2].wait()
    first_state = z_start(w_first, 0)
    def order_lines(part):
        lines = dot(
            order[part], lines_in[part].reshape(rows * 2 * quarter, pixels)
        ).astype(BF16)
        for f in range(quarter):
            for g in range(groups):
                left[g * token_rows : (g + 1) * token_rows, 128 * f : 128 * f + 128] = lines[
                    f * token_rows : (f + 1) * token_rows, 128 * g : 128 * g + 128
                ]

    depth = quarter * 128

    def stem_dot(part, v):
        at = pl.ds(pl.multiple_of(part * depth, depth), depth)
        return dot(left[...], wide[at, v * width : (v + 1) * width])

    for copy in over_core:
        copy.wait_recv()
    order_lines(half)
    last_lines = []
    for d, copy in zip(far_first, over_x):
        copy.wait_recv()
        slot = lax.rem(r + rows - d, rows)
        last_lines.append(pass_line(slot, 1 - half, 3, d, core_peer))
    for v in range(VARIANTS):
        stem_sum[:, v * width : (v + 1) * width] = stem_dot(half, v)
    for copy in last_lines:
        copy.wait_recv()
    order_lines(1 - half)
    z_pass(first_state)

    each = groups * TROWS
    row = iota((rows * each, 1), 0)
    strip, group, inner = over(row, each), over(row & (each - 1), TROWS), row & (TROWS - 1)
    turn = iota((rows * each, rows * each), 1) == group * token_rows + strip * TROWS + inner
    turn = turn.astype(BF16)
    part_copies = []

    def send_sums(k, sums):
        sums = jnp.concatenate(sums, axis=1).astype(BF16)
        part_out[k] = dot(turn, sums).astype(BF16).reshape(part_out.shape[1:])
        for d in far_first:
            to = lax.rem(r + d, rows)
            part_copies.append(
                remote(
                    part_out.at[k, to],
                    part_in.at[k, r],
                    part_s.at[k, d],
                    part_r.at[k, d],
                    (to, h),
                )
            )
        part_in[k, r] = part_out[k, r]

    def both(v):
        return stem_sum[:, v * width : (v + 1) * width] + stem_dot(1 - half, v)

    send_sums(0, [both(0), both(1)])
    rim = both(4)
    rim = jnp.concatenate([rim[token_rows:], jnp.zeros((token_rows, width), F32)], axis=0)
    send_sums(1, [both(2), both(3) + rim])
    loads[4].wait()
    query_state = z_start(w_query, 1, over_y=False)

    def norm(x, gain_ref):
        average = jnp.mean(x, axis=-1, keepdims=True)
        centered = x - average
        variance = jnp.mean(centered * centered, axis=-1, keepdims=True)
        return (centered * lax.rsqrt(variance + epsilon) * gain_ref[...].astype(F32).reshape(1, -1)).astype(
            BF16
        )

    z_end(first_state)
    for copy in loads[6:]:
        copy.wait()
    latent_norm[...] = norm(latent_rows[...].astype(F32), latent_gain)
    for copy in part_copies:
        copy.wait_recv()
    total = jnp.sum(part_in[...].astype(F32), axis=1)
    feature[h] = jnp.concatenate(
        [total[k, :, v * width : (v + 1) * width] for k in range(2) for v in range(2)], axis=0
    ).astype(BF16)

    feat_copies = []
    for d in range(1, heads):
        feat_copies.append(
            remote(
                feature.at[h],
                feature.at[h],
                feat_s.at[d],
                feat_r.at[d],
                (r, lax.rem(h + d, heads)),
            )
        )
    loads[5].wait()
    out_state = z_start(w_out, 2)
    z_pass(query_state)
    gather_wait(first_state[2:])
    for copy in feat_copies:
        copy.wait_recv()
    token_norm = norm(
        jnp.concatenate([feature[k] for k in range(heads)], axis=1).astype(F32), token_gain
    )
    kv_states = []
    for k in range(2):
        kv[k, r] = dot(token_norm, w_first[:, k].reshape(D, width)).astype(BF16)
        kv_states.append(gather_start(kv.at[k], k))
    z_end(query_state)
    depth = wq_ref.shape[0]
    part = jnp.zeros((2 * own, width), F32)
    for k in range(rows // 2):
        at = 2 * k + y
        part = part + dot(
            latent_norm[:, pl.ds(pl.multiple_of(at * depth, depth), depth)], w_query[at]
        )
    query_part[...] = part.reshape(query_part.shape)
    query_copy = remote(query_part.at[1 - y], query_in, query_s, query_r, (y_peer, h))
    z_pass(out_state)
    gather_forward(kv.at[0], 0, kv_states[0])
    query_copy.wait_recv()
    queries = (query_part[y] + query_in[...]).astype(BF16)
    gather_wait(kv_states[0])

    tokens = rows * kv.shape[2]
    keys = kv[0].reshape(tokens, width)
    size = D // HEADS
    side = iota((own, 128), 1) < size
    weights, totals = [], []
    for pair in range(width // 128):
        cols = slice(128 * pair, 128 * pair + 128)
        q = queries[:, cols].astype(F32)
        mine = jnp.concatenate([jnp.where(side, q, 0.0), jnp.where(side, 0.0, q)], axis=0)
        scores = lax.dot_general(
            mine.astype(BF16),
            keys[:, cols],
            (((1,), (1,)), ((), ())),
            preferred_element_type=F32,
        ) * size ** (-0.5)
        weight = jnp.exp(scores - jnp.max(scores, axis=1, keepdims=True))
        weights.append(weight.astype(BF16))
        totals.append(jnp.sum(weight, axis=1, keepdims=True))
    gather_forward(kv.at[1], 1, kv_states[1])
    z_end(out_state)
    gather_wait(kv_states[1])
    values = kv[1].reshape(tokens, width)
    mixed = []
    for pair in range(width // 128):
        v = values[:, 128 * pair : 128 * pair + 128]
        attended = dot(weights[pair], v) / totals[pair]
        mixed.append(jnp.where(side, attended[:own], attended[own:]).astype(BF16))
    mixed = jnp.concatenate(mixed, axis=1)

    gather_wait(out_state[2:])
    per_head = w_out.shape[0] // heads

    def out_term(k):
        block = w_out[pl.ds(per_head * k, per_head)].reshape(width, width)
        return lax.dot_general(
            mixed, block, (((1,), (1,)), ((), ())), preferred_element_type=F32
        )

    for k in range(heads):
        out_terms[k] = out_term(k).astype(BF16)
    end_copies = []
    for d in range(1, heads):
        to = lax.rem(h + d, heads)
        end_copies.append(
            remote(out_terms.at[to], out_in.at[d - 1], end_s.at[d], end_r.at[d], (r, to))
        )
    result = out_term(h)
    for d, copy in enumerate(end_copies, 1):
        copy.wait_recv()
        result = result + out_in[d - 1].astype(F32)
    out_ref[...] = result.astype(BF16)
    for copy in started:
        copy.wait_send()


def fused(rows, heads):
    def per_chip(imagery, stem, token_gain, latents, latent_gain, wq, wk, wv, wo):
        per = stem.shape[0] // KER
        pad = -(-per // 16) * 16
        width = stem.shape[1]
        pixels = imagery.shape[2]
        groups = pixels // 128
        own = latents.shape[0] // rows
        tokens = TROWS * TCOLS
        token_rows = rows * TROWS
        dma = pltpu.SemaphoreType.DMA
        return pl.pallas_call(
            functools.partial(strip_kernel, rows, heads),
            out_shape=jax.ShapeDtypeStruct((own, width), BF16),
            in_specs=[pl.BlockSpec(memory_space=pltpu.HBM)] * 9,
            out_specs=pl.BlockSpec(memory_space=pltpu.VMEM),
            scratch_shapes=[
                pltpu.VMEM(imagery.shape, BF16),
                pltpu.VMEM(stem.shape, BF16),
                pltpu.VMEM((D,), BF16),
                pltpu.VMEM((D,), BF16),
                pltpu.VMEM((2 * own, D), BF16),
                pltpu.VMEM((2 * own, D), BF16),
                pltpu.VMEM((2, own, width), F32),
                pltpu.VMEM((own, width), F32),
                pltpu.VMEM((rows, pad // 2, pixels), BF16),
                pltpu.VMEM((2, rows, 2, pad // 2, pixels), BF16),
                pltpu.VMEM((pad * 128, VARIANTS * width), BF16),
                pltpu.VMEM((2, pad // 2 * token_rows, rows * pad), BF16),
                pltpu.VMEM((groups * token_rows, pad // 2 * 128), BF16),
                pltpu.VMEM((groups * token_rows, VARIANTS * width), F32),
                pltpu.VMEM((2, rows, groups * TROWS, 2 * width), BF16),
                pltpu.VMEM((2, rows, groups * TROWS, 2 * width), BF16),
                pltpu.VMEM((heads, tokens, width), BF16),
                pltpu.VMEM((rows, 2, wk.shape[0], width), BF16),
                pltpu.VMEM((rows, wq.shape[0], width), BF16),
                pltpu.VMEM((rows, wo.shape[0], width), BF16),
                pltpu.VMEM((2, rows, tokens, width), BF16),
                pltpu.VMEM((heads, own, width), BF16),
                pltpu.VMEM((heads - 1, own, width), BF16),
                dma((9,)),
                dma((4, rows)),
                dma((4, rows)),
                dma,
                dma,
                dma((2, rows)),
                dma((2, rows)),
                dma((heads,)),
                dma((heads,)),
                dma((heads,)),
                dma((heads,)),
                dma((3, 3)),
                dma((3, 3)),
                dma((2, rows // 2)),
                dma((2, rows // 2)),
                dma((5, rows // 2)),
                dma((5, rows // 2)),
            ],
            compiler_params=pltpu.CompilerParams(
                collective_id=0, has_side_effects=True, vmem_limit_bytes=60 * 2**20
            ),
        )(
            imagery,
            stem,
            token_gain,
            latents,
            latent_gain,
            wq,
            wk,
            wv,
            wo,
        )

    return per_chip


def lines_fit(mesh):
    return mesh.shape["rows"] == 8 and mesh.shape["heads"] == 4


def solution(mesh):
    body = fused(mesh.shape["rows"], mesh.shape["heads"]) if lines_fit(mesh) else per_device
    return jax.shard_map(
        body,
        mesh=mesh,
        in_specs=(
            P(None, "rows", None),
            P("rows", "heads"),
            P(),
            P(),
            P(),
            P("rows", "heads"),
            P("rows", "heads"),
            P("rows", "heads"),
            P("rows", "heads"),
        ),
        out_specs=P("rows", "heads"),
        check_vma=False,
    )
```

```python
import functools

import jax
import jax.numpy as jnp
from jax import lax
from jax.experimental import pallas as pl
from jax.experimental.pallas import tpu as pltpu
from jax.sharding import PartitionSpec as P

D = 1024
HEADS = 16
LAT = 512
BANDS = 5
KER = 48
STRIDE = 32
TROWS = 2
TCOLS = 32


epsilon = 1e-05


def shifted(block, axis, distance):
    devices = range(lax.axis_size(axis))
    route = [(i - distance, i) for i in devices if i - distance in devices]
    return lax.ppermute(block, axis, route)


def layer_norm(inputs, gain_row):
    widened = inputs.astype(jnp.float32)
    average = jnp.mean(widened, axis=-1, keepdims=True)
    centered = widened - average
    variance = jnp.mean(centered * centered, axis=-1, keepdims=True)
    return (centered * lax.rsqrt(variance + epsilon) * gain_row.astype(jnp.float32)).astype(
        jnp.bfloat16
    )


def build_patches(strip_rows):
    rim_rows = KER - STRIDE
    padded = jnp.pad(strip_rows, ((0, 0), (0, STRIDE - rim_rows), (0, STRIDE)))
    blocks = padded.reshape(BANDS, TROWS + 1, STRIDE, TCOLS + 1, STRIDE)
    row_cat = jnp.concatenate([blocks[:, :TROWS], blocks[:, 1:, :rim_rows]], axis=2)
    col_cat = jnp.concatenate(
        [row_cat[:, :, :, :TCOLS, :], row_cat[:, :, :, 1:, :rim_rows]], axis=4
    )
    ordered = jnp.transpose(col_cat, (1, 3, 0, 2, 4))
    return ordered.reshape(TROWS * TCOLS, BANDS * KER * KER)


def per_device(
    imagery,
    stem_weight,
    token_gain,
    latents,
    latent_gain,
    query_weight,
    key_weight,
    value_weight,
    out_weight,
):
    rim_rows = KER - STRIDE
    below = shifted(imagery[:, :rim_rows, :], "rows", -1)
    patches = build_patches(jnp.concatenate([imagery, below], axis=1))
    token_count = patches.shape[0]
    width_dev = stem_weight.shape[1]
    stem_out = jnp.dot(
        patches,
        lax.all_gather(stem_weight, "rows", axis=0, tiled=True),
        preferred_element_type=jnp.float32,
    )
    feature = lax.all_gather(stem_out.astype(jnp.bfloat16), "heads", axis=1, tiled=True)
    token_norm = layer_norm(feature, token_gain)
    w_query, w_key, w_value, w_out = (
        lax.all_gather(query_weight, "rows", axis=0, tiled=True),
        lax.all_gather(key_weight, "rows", axis=0, tiled=True),
        lax.all_gather(value_weight, "rows", axis=0, tiled=True),
        lax.all_gather(out_weight, "rows", axis=0, tiled=True),
    )
    keys = jnp.dot(token_norm, w_key, preferred_element_type=jnp.float32).astype(jnp.bfloat16)
    values = jnp.dot(token_norm, w_value, preferred_element_type=jnp.float32).astype(jnp.bfloat16)
    head_size = D // HEADS
    heads_dev = width_dev // head_size
    latent_dev = LAT // lax.axis_size("rows")
    first_latent = lax.axis_index("rows") * latent_dev
    queries = jnp.dot(
        layer_norm(latents, latent_gain), w_query, preferred_element_type=jnp.float32
    ).astype(jnp.bfloat16)
    query_split = queries.reshape(LAT, heads_dev, head_size)
    key_split = keys.reshape(token_count, heads_dev, head_size)
    value_split = values.reshape(token_count, heads_dev, head_size)
    scores = jnp.einsum(
        "lhd,thd->lht", query_split, key_split, preferred_element_type=jnp.float32
    ) * head_size ** (-0.5)
    local_peak = jnp.max(scores, axis=2)

    def own_slice(array):
        return lax.dynamic_slice_in_dim(array, first_latent, latent_dev, 0)

    global_peak = lax.pmax(local_peak, "rows")
    weights = jnp.exp(scores - global_peak[:, :, None])
    totals = jnp.sum(weights, axis=2)
    upper_part = weights.astype(jnp.bfloat16)
    lower_part = (weights - upper_part.astype(jnp.float32)).astype(jnp.bfloat16)
    numerator = jnp.einsum(
        "lht,thd->lhd", upper_part, value_split, preferred_element_type=jnp.float32
    )
    numerator = numerator + jnp.einsum(
        "lht,thd->lhd", lower_part, value_split, preferred_element_type=jnp.float32
    )
    totals, numerator = (totals, numerator.reshape(LAT, width_dev))
    totals, numerator = lax.psum((totals, numerator), "rows")
    totals = own_slice(totals)
    numerator = own_slice(numerator)
    attended = numerator.reshape(latent_dev, heads_dev, head_size) / totals[:, :, None]
    mixed = attended.reshape(latent_dev, width_dev).astype(jnp.bfloat16)
    out_terms = lax.dot_general(
        mixed, w_out, (((1,), (1,)), ((), ())), preferred_element_type=jnp.float32
    )
    return lax.psum_scatter(out_terms, "heads", scatter_dimension=1, tiled=True).astype(
        jnp.bfloat16
    )


MESH = pl.DeviceIdType.MESH
VARIANTS = 5
F32 = jnp.float32
BF16 = jnp.bfloat16


def dot(a, b):
    return jnp.dot(a, b, preferred_element_type=F32)


def iota(shape, dim):
    return lax.broadcasted_iota(jnp.int32, shape, dim)


def over(index, power):
    return lax.shift_right_logical(index, power.bit_length() - 1)


def band_and_line(flat):
    band = jnp.zeros_like(flat)
    for step in range(1, BANDS + 1):
        band = band + (flat >= KER * step).astype(jnp.int32)
    return band, flat - KER * band


def strip_kernel(
    rows,
    heads,
    image_ref,
    stem_ref,
    token_gain_ref,
    latents_ref,
    latent_gain_ref,
    wq_ref,
    wk_ref,
    wv_ref,
    wo_ref,
    out_ref,
    image,
    stem,
    token_gain,
    latent_gain,
    latent_rows,
    latent_norm,
    query_part,
    query_in,
    lines_out,
    lines_in,
    wide,
    order,
    left,
    stem_sum,
    part_out,
    part_in,
    feature,
    w_key,
    w_value,
    w_query,
    w_out,
    kv,
    out_terms,
    out_in,
    local,
    line_s,
    line_r,
    query_s,
    query_r,
    part_s,
    part_r,
    feat_s,
    feat_r,
    end_s,
    end_r,
    z_s,
    z_r,
    gz_s,
    gz_r,
    gy_s,
    gy_r,
):
    r = lax.axis_index("rows")
    h = lax.axis_index("heads")
    core = lax.rem(h, 2)
    core_peer = h + 1 - 2 * core
    half = h // 2
    x_peer = lax.rem(h + 2, heads)
    y = lax.rem(r, 2)
    z = r // 2
    y_peer = r + 1 - 2 * y
    z_opposite = lax.rem(r + 4, rows)
    z_pair = r + 2 - 4 * lax.rem(z, 2)
    z_last = lax.rem(z_pair + 4, rows)
    own = latents_ref.shape[0] // rows
    per = stem_ref.shape[0] // KER
    quarter = lines_in.shape[3]
    width = stem_ref.shape[1]
    pixels = image_ref.shape[2]
    groups = pixels // 128
    started = []

    loads = [
        pltpu.make_async_copy(source, target, local.at[k])
        for k, (source, target) in enumerate(
            [
                (image_ref, image),
                (wk_ref, w_key.at[r]),
                (wv_ref, w_value.at[r]),
                (stem_ref, stem),
                (wq_ref, w_query.at[r]),
                (wo_ref, w_out.at[r]),
                (
                    latents_ref.at[pl.ds(pl.multiple_of(z * 2 * own, 2 * own), 2 * own)],
                    latent_rows,
                ),
                (token_gain_ref, token_gain),
                (latent_gain_ref, latent_gain),
            ]
        )
    ]
    for copy in loads:
        copy.start()

    barrier = pltpu.get_barrier_semaphore()
    for d in range(1, rows):
        pl.semaphore_signal(
            barrier, inc=1, device_id=(lax.rem(r + d, rows), h), device_id_type=MESH
        )
    for d in range(1, heads):
        pl.semaphore_signal(
            barrier, inc=1, device_id=(r, lax.rem(h + d, heads)), device_id_type=MESH
        )

    height = image_ref.shape[1]

    def pick(receiver, second, line):
        band, at = band_and_line(per * receiver + line)
        source = band * height + ((at + STRIDE * second) & (height - 1))
        places = iota((source.shape[0], BANDS * height), 1)
        flat = image[...].reshape(BANDS * height, pixels)
        return dot((places == source).astype(BF16), flat).astype(BF16)

    row = iota((rows * quarter, 1), 0)
    wide[...] = jnp.zeros_like(wide)
    loads[0].wait()
    lines_out[...] = pick(over(row, quarter), core, half * quarter + (row & (quarter - 1))).reshape(
        lines_out.shape
    )
    pl.semaphore_wait(barrier, rows - 1 + heads - 1)

    def remote(src, dst, send, recv, to):
        copy = pltpu.make_async_remote_copy(
            src_ref=src,
            dst_ref=dst,
            send_sem=send,
            recv_sem=recv,
            device_id=to,
            device_id_type=MESH,
        )
        copy.start()
        started.append(copy)
        return copy

    def gather_start(buf, which):
        first = [
            remote(
                buf.at[r],
                buf.at[r],
                gz_s.at[which, d],
                gz_r.at[which, d],
                (lax.rem(r + 2 * d, rows), h),
            )
            for d in range(1, rows // 2)
        ]
        across = remote(
            buf.at[r], buf.at[r], gy_s.at[4 + which, 0], gy_r.at[4 + which, 0], (y_peer, h)
        )
        return first, [across]

    def gather_forward(buf, which, state):
        first, across = state
        for d, copy in enumerate(first, 1):
            copy.wait_recv()
            slot = lax.rem(r + rows - 2 * d, rows)
            across.append(
                remote(
                    buf.at[slot],
                    buf.at[slot],
                    gy_s.at[4 + which, d],
                    gy_r.at[4 + which, d],
                    (y_peer, h),
                )
            )

    def gather_wait(state):
        for copy in state[1]:
            copy.wait_recv()

    def z_start(buf, which, over_y=True):
        own_slot = buf.at[r]
        pair = remote(
            own_slot, own_slot, z_s.at[which, 1], z_r.at[which, 1], (z_pair, h)
        )
        across = []

        def y_send(slot):
            k = len(across)
            if over_y:
                ref = buf.at[slot]
                across.append(
                    remote(ref, ref, gy_s.at[which, k], gy_r.at[which, k], (y_peer, h))
                )

        y_send(r)
        return {"buf": buf, "which": which, "pair": pair, "across": across, "y": y_send}

    def z_far(state):
        ref, which = state["buf"].at[r], state["which"]
        state["far"] = remote(
            ref, ref, z_s.at[which, 0], z_r.at[which, 0], (z_opposite, h)
        )

    def z_near_pass(state):
        state["pair"].wait_recv()
        state["y"](z_pair)

    def z_far_pass(state):
        which = state["which"]
        state["far"].wait_recv()
        ref = state["buf"].at[z_opposite]
        state["last"] = remote(ref, ref, z_s.at[which, 2], z_r.at[which, 2], (z_pair, h))
        state["y"](z_opposite)

    def z_end(state):
        state["last"].wait_recv()
        state["y"](z_last)

    def all_in(state):
        for copy in state["across"]:
            copy.wait_recv()

    far_first = (4, 3, 5, 2, 6, 1, 7)
    line_copies = []
    for d in far_first:
        to = lax.rem(r + d, rows)
        line_copies.append(
            remote(
                lines_out.at[to],
                lines_in.at[half, r, core],
                line_s.at[0, d],
                line_r.at[0, d],
                (to, h),
            )
        )
    loads[1].wait()
    loads[2].wait()
    first_states = [z_start(w_key, 0), z_start(w_value, 3)]
    for part in range(2):
        row = iota((2 * quarter, 1), 0)
        lines_in[part, r] = pick(
            r, over(row, quarter), part * quarter + (row & (quarter - 1))
        ).reshape(2, quarter, pixels)
    def widen(f, carry):
        block = stem[pl.ds(pl.multiple_of(f * KER, 16), KER), :]
        for v in range(VARIANTS - 2):
            wide[
                pl.ds(pl.multiple_of(f * 128 + STRIDE * v, 16), KER),
                v * width : (v + 1) * width,
            ] = block
        v = VARIANTS - 2
        wide[
            pl.ds(pl.multiple_of(f * 128 + STRIDE * v, 16), STRIDE),
            v * width : (v + 1) * width,
        ] = block[:STRIDE]
        v = VARIANTS - 1
        wide[
            pl.ds(pl.multiple_of(f * 128, 16), KER - STRIDE), v * width : (v + 1) * width
        ] = block[STRIDE:]
        return carry

    token_rows = rows * TROWS
    row = iota((quarter * token_rows, 1), 0)
    line, token_row = over(row, token_rows), row & (token_rows - 1)
    odd = token_row & 1
    for part in range(2):
        _, at = band_and_line(per * r + part * quarter + line)
        strip = over(token_row, 2) + jnp.where((odd == 1) & (at >= STRIDE), 1, 0)
        target = (strip * 2 + odd) * quarter + line
        order[part] = (iota(order.shape[1:], 1) == target).astype(BF16)

    def pass_line(slot, part, k, d, to):
        ref = lines_in.at[part, slot, core]
        return remote(ref, ref, line_s.at[k, d], line_r.at[k, d], (r, to))

    over_x, over_core = [], []
    loads[3].wait()
    parts = len(far_first)
    for k, (d, copy) in enumerate(zip(far_first, line_copies)):
        lax.fori_loop(per * k // parts, per * (k + 1) // parts, widen, 0)
        copy.wait_recv()
        slot = lax.rem(r + rows - d, rows)
        over_x.append(pass_line(slot, half, 1, d, x_peer))
        over_core.append(pass_line(slot, half, 2, d, core_peer))
    for state in first_states:
        z_far(state)
        z_near_pass(state)
    def order_lines(part):
        lines = dot(
            order[part], lines_in[part].reshape(rows * 2 * quarter, pixels)
        ).astype(BF16)
        for f in range(quarter):
            for g in range(groups):
                left[g * token_rows : (g + 1) * token_rows, 128 * f : 128 * f + 128] = lines[
                    f * token_rows : (f + 1) * token_rows, 128 * g : 128 * g + 128
                ]

    depth = quarter * 128

    def stem_dot(part, v):
        at = pl.ds(pl.multiple_of(part * depth, depth), depth)
        return dot(left[...], wide[at, v * width : (v + 1) * width])

    for copy in over_core:
        copy.wait_recv()
    order_lines(half)
    last_lines = []
    for d, copy in zip(far_first, over_x):
        copy.wait_recv()
        slot = lax.rem(r + rows - d, rows)
        last_lines.append(pass_line(slot, 1 - half, 3, d, core_peer))
    for v in range(VARIANTS):
        stem_sum[:, v * width : (v + 1) * width] = stem_dot(half, v)
    for copy in last_lines:
        copy.wait_recv()
    order_lines(1 - half)
    for state in first_states:
        z_far_pass(state)

    each = groups * TROWS
    row = iota((rows * each, 1), 0)
    strip, group, inner = over(row, each), over(row & (each - 1), TROWS), row & (TROWS - 1)
    turn = iota((rows * each, rows * each), 1) == group * token_rows + strip * TROWS + inner
    turn = turn.astype(BF16)
    part_copies = []

    def send_sums(k, sums):
        sums = jnp.concatenate(sums, axis=1).astype(BF16)
        part_out[k] = dot(turn, sums).astype(BF16).reshape(part_out.shape[1:])
        for d in far_first:
            to = lax.rem(r + d, rows)
            part_copies.append(
                remote(
                    part_out.at[k, to],
                    part_in.at[k, r],
                    part_s.at[k, d],
                    part_r.at[k, d],
                    (to, h),
                )
            )
        part_in[k, r] = part_out[k, r]

    def both(v):
        return stem_sum[:, v * width : (v + 1) * width] + stem_dot(1 - half, v)

    send_sums(0, [both(0), both(1)])
    rim = both(4)
    rim = jnp.concatenate([rim[token_rows:], jnp.zeros((token_rows, width), F32)], axis=0)
    send_sums(1, [both(2), both(3) + rim])
    loads[4].wait()
    query_state = z_start(w_query, 1, over_y=False)
    z_far(query_state)

    def norm(x, gain_ref):
        average = jnp.mean(x, axis=-1, keepdims=True)
        centered = x - average
        variance = jnp.mean(centered * centered, axis=-1, keepdims=True)
        return (centered * lax.rsqrt(variance + epsilon) * gain_ref[...].astype(F32).reshape(1, -1)).astype(
            BF16
        )

    for state in first_states:
        z_end(state)
    for copy in loads[6:]:
        copy.wait()
    latent_norm[...] = norm(latent_rows[...].astype(F32), latent_gain)
    for copy in part_copies:
        copy.wait_recv()
    total = jnp.sum(part_in[...].astype(F32), axis=1)
    feature[h] = jnp.concatenate(
        [total[k, :, v * width : (v + 1) * width] for k in range(2) for v in range(2)], axis=0
    ).astype(BF16)

    feat_copies = []
    for d in range(1, heads):
        feat_copies.append(
            remote(
                feature.at[h],
                feature.at[h],
                feat_s.at[d],
                feat_r.at[d],
                (r, lax.rem(h + d, heads)),
            )
        )
    loads[5].wait()
    out_state = z_start(w_out, 2)
    z_far(out_state)
    z_near_pass(query_state)
    z_far_pass(query_state)
    all_in(first_states[0])
    for copy in feat_copies:
        copy.wait_recv()
    token_norm = norm(
        jnp.concatenate([feature[k] for k in range(heads)], axis=1).astype(F32), token_gain
    )
    kv_states = []
    for k, weight in enumerate((w_key, w_value)):
        if k == 1:
            all_in(first_states[1])
        kv[k, r] = dot(token_norm, weight[...].reshape(D, width)).astype(BF16)
        kv_states.append(gather_start(kv.at[k], k))
    z_end(query_state)
    depth = wq_ref.shape[0]
    part = jnp.zeros((2 * own, width), F32)
    for k in range(rows // 2):
        at = 2 * k + y
        part = part + dot(
            latent_norm[:, pl.ds(pl.multiple_of(at * depth, depth), depth)], w_query[at]
        )
    query_part[...] = part.reshape(query_part.shape)
    query_copy = remote(query_part.at[1 - y], query_in, query_s, query_r, (y_peer, h))
    z_near_pass(out_state)
    z_far_pass(out_state)
    gather_forward(kv.at[0], 0, kv_states[0])
    query_copy.wait_recv()
    queries = (query_part[y] + query_in[...]).astype(BF16)
    gather_wait(kv_states[0])

    tokens = rows * kv.shape[2]
    keys = kv[0].reshape(tokens, width)
    size = D // HEADS
    side = iota((own, 128), 1) < size
    weights, totals = [], []
    for pair in range(width // 128):
        cols = slice(128 * pair, 128 * pair + 128)
        q = queries[:, cols].astype(F32)
        mine = jnp.concatenate([jnp.where(side, q, 0.0), jnp.where(side, 0.0, q)], axis=0)
        scores = lax.dot_general(
            mine.astype(BF16),
            keys[:, cols],
            (((1,), (1,)), ((), ())),
            preferred_element_type=F32,
        ) * size ** (-0.5)
        weight = jnp.exp(scores - jnp.max(scores, axis=1, keepdims=True))
        weights.append(weight.astype(BF16))
        totals.append(jnp.sum(weight, axis=1, keepdims=True))
    gather_forward(kv.at[1], 1, kv_states[1])
    z_end(out_state)
    gather_wait(kv_states[1])
    values = kv[1].reshape(tokens, width)
    mixed = []
    for pair in range(width // 128):
        v = values[:, 128 * pair : 128 * pair + 128]
        attended = dot(weights[pair], v) / totals[pair]
        mixed.append(jnp.where(side, attended[:own], attended[own:]).astype(BF16))
    mixed = jnp.concatenate(mixed, axis=1)

    all_in(out_state)
    per_head = w_out.shape[0] // heads

    def out_term(k):
        block = w_out[pl.ds(per_head * k, per_head)].reshape(width, width)
        return lax.dot_general(
            mixed, block, (((1,), (1,)), ((), ())), preferred_element_type=F32
        )

    for k in range(heads):
        out_terms[k] = out_term(k).astype(BF16)
    end_copies = []
    for d in range(1, heads):
        to = lax.rem(h + d, heads)
        end_copies.append(
            remote(out_terms.at[to], out_in.at[d - 1], end_s.at[d], end_r.at[d], (r, to))
        )
    result = out_term(h)
    for d, copy in enumerate(end_copies, 1):
        copy.wait_recv()
        result = result + out_in[d - 1].astype(F32)
    out_ref[...] = result.astype(BF16)
    for copy in started:
        copy.wait_send()


def fused(rows, heads):
    def per_chip(imagery, stem, token_gain, latents, latent_gain, wq, wk, wv, wo):
        per = stem.shape[0] // KER
        pad = -(-per // 16) * 16
        width = stem.shape[1]
        pixels = imagery.shape[2]
        groups = pixels // 128
        own = latents.shape[0] // rows
        tokens = TROWS * TCOLS
        token_rows = rows * TROWS
        dma = pltpu.SemaphoreType.DMA
        return pl.pallas_call(
            functools.partial(strip_kernel, rows, heads),
            out_shape=jax.ShapeDtypeStruct((own, width), BF16),
            in_specs=[pl.BlockSpec(memory_space=pltpu.HBM)] * 9,
            out_specs=pl.BlockSpec(memory_space=pltpu.VMEM),
            scratch_shapes=[
                pltpu.VMEM(imagery.shape, BF16),
                pltpu.VMEM(stem.shape, BF16),
                pltpu.VMEM((D,), BF16),
                pltpu.VMEM((D,), BF16),
                pltpu.VMEM((2 * own, D), BF16),
                pltpu.VMEM((2 * own, D), BF16),
                pltpu.VMEM((2, own, width), F32),
                pltpu.VMEM((own, width), F32),
                pltpu.VMEM((rows, pad // 2, pixels), BF16),
                pltpu.VMEM((2, rows, 2, pad // 2, pixels), BF16),
                pltpu.VMEM((pad * 128, VARIANTS * width), BF16),
                pltpu.VMEM((2, pad // 2 * token_rows, rows * pad), BF16),
                pltpu.VMEM((groups * token_rows, pad // 2 * 128), BF16),
                pltpu.VMEM((groups * token_rows, VARIANTS * width), F32),
                pltpu.VMEM((2, rows, groups * TROWS, 2 * width), BF16),
                pltpu.VMEM((2, rows, groups * TROWS, 2 * width), BF16),
                pltpu.VMEM((heads, tokens, width), BF16),
                pltpu.VMEM((rows, wk.shape[0], width), BF16),
                pltpu.VMEM((rows, wv.shape[0], width), BF16),
                pltpu.VMEM((rows, wq.shape[0], width), BF16),
                pltpu.VMEM((rows, wo.shape[0], width), BF16),
                pltpu.VMEM((2, rows, tokens, width), BF16),
                pltpu.VMEM((heads, own, width), BF16),
                pltpu.VMEM((heads - 1, own, width), BF16),
                dma((9,)),
                dma((4, rows)),
                dma((4, rows)),
                dma,
                dma,
                dma((2, rows)),
                dma((2, rows)),
                dma((heads,)),
                dma((heads,)),
                dma((heads,)),
                dma((heads,)),
                dma((4, 3)),
                dma((4, 3)),
                dma((2, rows // 2)),
                dma((2, rows // 2)),
                dma((6, rows // 2)),
                dma((6, rows // 2)),
            ],
            compiler_params=pltpu.CompilerParams(
                collective_id=0, has_side_effects=True, vmem_limit_bytes=60 * 2**20
            ),
        )(
            imagery,
            stem,
            token_gain,
            latents,
            latent_gain,
            wq,
            wk,
            wv,
            wo,
        )

    return per_chip


def lines_fit(mesh):
    return mesh.shape["rows"] == 8 and mesh.shape["heads"] == 4


def solution(mesh):
    body = fused(mesh.shape["rows"], mesh.shape["heads"]) if lines_fit(mesh) else per_device
    return jax.shard_map(
        body,
        mesh=mesh,
        in_specs=(
            P(None, "rows", None),
            P("rows", "heads"),
            P(),
            P(),
            P(),
            P("rows", "heads"),
            P("rows", "heads"),
            P("rows", "heads"),
            P("rows", "heads"),
        ),
        out_specs=P("rows", "heads"),
        check_vma=False,
    )
```
